256 devices in a mesh: dp: 16 (over x, y_lo, core), tensor: 16 (over z, y_hi).
Axes of the slice: x: 4, y: 4 (y_hi: 2, y_lo: 2; y = y_hi * 2 + y_lo), z: 8, core: 2. Of those that a mesh axis runs over, the one named last changes fastest.
Arguments:
- tokens: bfloat16 [16, 128, 8192], P('dp', None, 'tensor'), may hold values from -6 to 6
- norm_gain: bfloat16 [8192], P('tensor'), may hold values from 0.5 to 1.5
- w_query: bfloat16 [8192, 4096], P(None, 'tensor'), may hold values from -0.0625 to 0.0625
- w_key: bfloat16 [8192, 512], P(None, 'tensor'), may hold values from -0.0625 to 0.0625
- w_value: bfloat16 [8192, 512], P(None, 'tensor'), may hold values from -0.0625 to 0.0625
- w_output: bfloat16 [4096, 8192], P('tensor'), may hold values from -0.09375 to 0.09375
- positions: int32 [16, 128], P('dp'), may hold values from 0 to 127, as said below
- scale_exps: int32 [7], replicated, may hold values from 2 to 15, as said below
- loss_exp: int32 [1], replicated, may hold values from 12 to 13
- out_grad: bfloat16 [16, 128, 8192], P('dp', None, 'tensor'), may hold values from -6 to 6
Outputs:
- mixed: bfloat16 [16, 128, 8192], P('dp', None, 'tensor')
- d_tokens: bfloat16 [16, 128, 8192], P('dp', None, 'tensor')
- grad_query: float32 [8192, 4096], P('dp', 'tensor')
- grad_key: float32 [8192, 512], P('dp', 'tensor')
- grad_value: float32 [8192, 512], P('dp', 'tensor')
- grad_output: float32 [4096, 8192], P('tensor', 'dp')
The draws below stay inside these ranges and needn't reach their ends.
Inputs may be any that keep to these rules, and one draw needn't show every extreme that they name: `positions`: in each group the first token's position is 0 and every other token's position is 0 or the previous token's plus one. `scale_exps`: entries belong in order to the casts of normed, w_query, w_key, w_value, w_output, attended and the output gradient; entry 0 is 7 or 8, entries 1 to 4 are 14 or 15, entry 5 is 8 or 9, entry 6 is 2 or 3.
All inputs are finite; a program needn't handle non-finite values.
Results may differ from the reference program's by a relative error of at most 0.028.
Values may be sent and summed in bfloat16 or wider, within the bound.
A program may use at most 128 MiB of HBM per device.

```python
import math
import jax
import jax.numpy as jnp
from jax import lax

D = 8192
HD = 128
HEADS = 32
KV_HEADS = 4
TOKENS = 128
QW = 4096
KVW = 512
GROUPS = 16
N_TENSOR = 16


def draw_positions(key, part):
    key = jax.random.fold_in(key, 11)
    cuts = jax.random.randint(key, (GROUPS, 3), 0, TOKENS, dtype=jnp.int32)
    group_ids = jnp.arange(GROUPS, dtype=jnp.int32)
    cuts = jnp.where(group_ids[:, None] == 0, 0, cuts).astype(jnp.int32)
    places = jnp.arange(TOKENS, dtype=jnp.int32)
    starts = jnp.any(places[None, None, :] == cuts[:, :, None], axis=1) | (places[None, :] == 0)
    begin = lax.cummax(jnp.where(starts, places[None, :], 0), axis=1)
    return (places[None, :] - begin).astype(jnp.int32)


def draw_scale_exps(key, part):
    key = jax.random.fold_in(key, 23)
    base = jnp.array([7, 14, 14, 14, 14, 8, 2], dtype=jnp.int32)
    return base + jax.random.randint(key, (7,), 0, 2, dtype=jnp.int32)


def spiked(drawn, key, source, target, shards_of, factor):
    owner, partner = [(jnp.arange(drawn.shape[axis_at]) // (drawn.shape[axis_at] // shards_of)).reshape([-1 if axis == axis_at else 1 for axis in range(drawn.ndim)]) for axis_at in (source, target)]
    chosen = jax.random.permutation(key, shards_of)[partner]
    strong = (owner == chosen) | (owner == (partner + shards_of // 2) % shards_of)
    return jnp.where(strong, factor * drawn, drawn)


def levels(own_key, shape, cuts, smallest, top_value):
    def one(dim, parts):
        steps = jax.random.uniform(jax.random.fold_in(jax.random.fold_in(own_key, 6), dim), (parts,), jnp.float32, smallest / len(cuts), top_value / len(cuts))
        return jnp.repeat(jnp.exp(steps), shape[dim] // parts).reshape((-1,) + (1,) * (len(shape) - dim - 1))

    factor_of = one(*cuts[0])
    for cut in cuts[1:]:
        factor_of = factor_of * one(*cut)
    return factor_of


def scatter_about(rng, extent, scale, reach, cuts=(), kind=jnp.bfloat16):
    entries = scale * jax.random.normal(rng, extent, jnp.float32)
    if cuts:
        entries = entries * levels(rng, extent, cuts, -0.22, 0.18)
    return jnp.clip(entries, -reach, reach).astype(kind)


def noise_with(key, dims, spread, most, cuts, heavy, kind=jnp.bfloat16):
    result = spread * jax.random.normal(key, dims, jnp.float32)
    if cuts:
        result = result * levels(key, dims, cuts, -0.22, 0.18)
    return jnp.clip(spiked(result, jax.random.fold_in(key, 3), *heavy), -most, most).astype(kind)


def setup_inputs(seed: int = 0) -> dict:
    streams_of = jax.random.split(jax.random.key(seed), 11)
    tokens = noise_with(streams_of[0], (GROUPS, TOKENS, D), 1.0, 6.0, ((0, 16), (2, 16)), (0, 2, 16, 2.0))
    norm_gain = jnp.clip(1.0 + 0.1 * jax.random.normal(streams_of[1], (D,), jnp.float32), 0.5, 1.5).astype(jnp.bfloat16)
    w_query = scatter_about(streams_of[2], (D, QW), D ** -0.5, 0.0625, ((1, 16),))
    w_key = scatter_about(streams_of[3], (D, KVW), D ** -0.5, 0.0625, ((1, 16),))
    w_value = scatter_about(streams_of[4], (D, KVW), D ** -0.5, 0.0625, ((1, 16),))
    w_output = scatter_about(streams_of[5], (QW, D), QW ** -0.5, 0.09375, ((0, 16),))
    positions = draw_positions(jax.random.fold_in(streams_of[10], 71), 0)
    scale_exps = draw_scale_exps(jax.random.fold_in(streams_of[10], 71), 0)
    loss_exp = jax.random.randint(streams_of[8], (1,), 12, 14).astype(jnp.int32)
    out_grad = scatter_about(streams_of[9], (GROUPS, TOKENS, D), 1.0, 6.0, ((0, 16), (2, 16)))
    return dict(tokens=tokens, norm_gain=norm_gain, w_query=w_query, w_key=w_key, w_value=w_value, w_output=w_output, positions=positions, scale_exps=scale_exps, loss_exp=loss_exp, out_grad=out_grad)


HIGH = lax.Precision.HIGHEST
E4_TOP = 448.0
E5_TOP = 57344.0

def settle(values):
    return lax.optimization_barrier(values.astype(jnp.bfloat16))

def saturate(values, limit):
    return jnp.clip(values.astype(jnp.float32), -limit, limit)

def rms_norm(rows, gain):
    rows = rows.astype(jnp.float32)
    return rows * lax.rsqrt(lax.optimization_barrier(jnp.mean(rows * rows, axis=-1, keepdims=True)) + 1e-05) * gain.astype(jnp.float32)

def rotate(values, positions):
    half = values.shape[-1] // 2
    inverse = jnp.power(500000.0, -2.0 * jnp.arange(half, dtype=jnp.float32) / values.shape[-1])
    angles = positions.astype(jnp.float32)[:, None] * inverse[None, :]
    cosine = jnp.cos(angles)[:, None, :]
    sine = jnp.sin(angles)[:, None, :]
    first = values[..., :half]
    second = values[..., half:]
    return jnp.concatenate([first * cosine - second * sine, second * cosine + first * sine], axis=-1)

def probabilities(query, keys, positions):
    count = query.shape[0]
    scores = jnp.einsum('thd,shd->hts', rotate(query, positions), rotate(keys, positions), precision=HIGH) / math.sqrt(query.shape[-1])
    places = jnp.arange(count, dtype=jnp.int32)
    allowed = (places[None, :] <= places[:, None]) & (places[None, :] >= places[:, None] - positions[:, None])
    weights = jnp.where(allowed[None], jnp.exp(jnp.where(allowed[None], scores, 0.0)), 0.0)
    return weights / lax.optimization_barrier(jnp.sum(weights, axis=-1, keepdims=True))

def attention_core(query, keys, values, positions):
    return jnp.einsum('hts,shd->thd', probabilities(query, keys, positions), values, precision=HIGH)

def head_major(columns):
    count = columns.shape[0]
    return jnp.transpose(columns.reshape(count, HD, KV_HEADS), (0, 2, 1))

def feature_major(heads):
    count = heads.shape[0]
    return jnp.transpose(heads, (0, 2, 1)).reshape(count, KVW)

def reference(tokens, norm_gain, w_query, w_key, w_value, w_output, positions, scale_exps, loss_exp, out_grad):
    limits = E4_TOP * jnp.exp2(-scale_exps.astype(jnp.float32))
    grad_top = E5_TOP * jnp.exp2(-(scale_exps[6] + loss_exp[0]).astype(jnp.float32))
    query_cast = saturate(w_query, limits[1]).astype(jnp.bfloat16)
    key_cast = saturate(w_key, limits[2]).astype(jnp.bfloat16)
    value_cast = saturate(w_value, limits[3]).astype(jnp.bfloat16)
    output_cast = saturate(w_output, limits[4]).astype(jnp.bfloat16)
    sharing = HEADS // KV_HEADS
    qsplit = QW // N_TENSOR
    ksplit = KVW // N_TENSOR

    def one_group(carry, inputs):
        rows, grad_rows, place = inputs
        count = rows.shape[0]
        acts = saturate(rms_norm(rows, norm_gain), limits[0]).astype(jnp.bfloat16)
        query = jnp.dot(acts, query_cast, preferred_element_type=jnp.float32).astype(jnp.bfloat16)
        keys = jnp.dot(acts, key_cast, preferred_element_type=jnp.float32).astype(jnp.bfloat16)
        values = jnp.dot(acts, value_cast, preferred_element_type=jnp.float32).astype(jnp.bfloat16)
        query_h = query.astype(jnp.float32).reshape(count, HEADS, HD)
        keys_h = jnp.repeat(head_major(keys.astype(jnp.float32)), sharing, axis=1)
        values_h = jnp.repeat(head_major(values.astype(jnp.float32)), sharing, axis=1)
        weights = settle(probabilities(query_h, keys_h, place)).astype(jnp.float32)
        attended = jnp.einsum('hts,shd->thd', weights, values_h, precision=HIGH).reshape(count, QW).astype(jnp.bfloat16)
        attended = saturate(attended, limits[5]).astype(jnp.bfloat16)
        pieces = jnp.einsum('tkc,kcd->ktd', attended.astype(jnp.float32).reshape(count, N_TENSOR, qsplit), output_cast.astype(jnp.float32).reshape(N_TENSOR, qsplit, D), precision=HIGH)
        mixed = lax.optimization_barrier(jnp.sum(settle(pieces).astype(jnp.float32), axis=0)).astype(jnp.bfloat16)
        grad_cast = saturate(grad_rows, grad_top).astype(jnp.bfloat16)
        d_att = jnp.dot(grad_cast, output_cast.T, preferred_element_type=jnp.float32).astype(jnp.bfloat16)
        _, pullback = jax.vjp(lambda left, middle, right: attention_core(left, middle, right, place), query_h, keys_h, values_h)
        d_query_h, d_keys_h, d_values_h = pullback(d_att.astype(jnp.float32).reshape(count, HEADS, HD))
        d_query = d_query_h.reshape(count, QW).astype(jnp.bfloat16)
        d_keys = feature_major(lax.optimization_barrier(jnp.sum(d_keys_h.reshape(count, KV_HEADS, sharing, HD), axis=2))).astype(jnp.bfloat16)
        d_values = feature_major(lax.optimization_barrier(jnp.sum(d_values_h.reshape(count, KV_HEADS, sharing, HD), axis=2))).astype(jnp.bfloat16)
        part_query = jnp.einsum('tkc,dkc->ktd', d_query.astype(jnp.float32).reshape(count, N_TENSOR, qsplit), query_cast.astype(jnp.float32).reshape(D, N_TENSOR, qsplit), precision=HIGH)
        part_key = jnp.einsum('tkc,dkc->ktd', d_keys.astype(jnp.float32).reshape(count, N_TENSOR, ksplit), key_cast.astype(jnp.float32).reshape(D, N_TENSOR, ksplit), precision=HIGH)
        part_value = jnp.einsum('tkc,dkc->ktd', d_values.astype(jnp.float32).reshape(count, N_TENSOR, ksplit), value_cast.astype(jnp.float32).reshape(D, N_TENSOR, ksplit), precision=HIGH)
        d_normed = lax.optimization_barrier(jnp.sum(settle(part_query + part_key + part_value).astype(jnp.float32), axis=0))
        _, norm_back = jax.vjp(lambda inner: rms_norm(inner, norm_gain), rows.astype(jnp.float32))
        d_rows = norm_back(d_normed)[0].astype(jnp.bfloat16)
        carry = (carry[0] + jnp.dot(acts.T, d_query, preferred_element_type=jnp.float32), carry[1] + jnp.dot(acts.T, d_keys, preferred_element_type=jnp.float32), carry[2] + jnp.dot(acts.T, d_values, preferred_element_type=jnp.float32), carry[3] + jnp.dot(attended.T, grad_cast, preferred_element_type=jnp.float32))
        return (carry, (mixed, d_rows))
    start = (jnp.zeros((D, QW), jnp.float32), jnp.zeros((D, KVW), jnp.float32), jnp.zeros((D, KVW), jnp.float32), jnp.zeros((QW, D), jnp.float32))
    sums, (mixed, d_tokens) = lax.scan(one_group, start, (tokens, out_grad, positions))
    return (mixed, d_tokens, sums[0], sums[1], sums[2], sums[3])
```

```python
import functools
import math

import jax
import jax.numpy as jnp
from jax import lax
from jax.experimental import pallas as pl
from jax.experimental.pallas import tpu as pltpu
from jax.sharding import PartitionSpec as P

HD = 128
E4_TOP = 448.0
E5_TOP = 57344.0
BF = jnp.bfloat16
F32 = jnp.float32
MESH = pl.DeviceIdType.MESH
NZ, NX, TOK, FEAT, QC, KC = 8, 4, 128, 512, 256, 32
DIRS = (1, -1)


def nn(a, b):
    return jnp.dot(a, b, preferred_element_type=F32)


def nt(a, b):
    return lax.dot_general(a, b, (((1,), (1,)), ((), ())), preferred_element_type=F32)


def halves(a):
    high = a.astype(BF)
    return high, (a - high.astype(F32)).astype(BF)


def precise(dot, a, b):
    ah, al = halves(a)
    bh, bl = halves(b)
    return dot(ah, bh) + (dot(ah, bl) + dot(al, bh))


def power_of_half(e):
    out = jnp.float32(1.0)
    for bit in range(5):
        out = out * jnp.where(((e >> bit) & 1) == 1, jnp.float32(2.0 ** -(1 << bit)), jnp.float32(1.0))
    return out


def clip(v, limit):
    return jnp.minimum(jnp.maximum(v, -limit), limit)


def rot(v, c, s):
    return jnp.concatenate([v[:64] * c - v[64:] * s, v[64:] * c + v[:64] * s], axis=0)


def unrot(v, c, s):
    return jnp.concatenate([v[:64] * c + v[64:] * s, v[64:] * c - v[:64] * s], axis=0)


def kernel(
    scale_ref, loss_ref, tok_ref, gain_ref, pos_ref, og_ref, wq_hbm, wk_hbm, wv_hbm, wo_hbm,
    mixed_ref, dtok_ref, gqkv_ref, go_ref,
    wq, wk, wv, wo, acts, gout, pacts, pgout,
    pm, rm, ym, pd, rd, yd,
    sgo, xgo, ygo, sgq, xgq, ygq,
    att_own, att_far, dq_own, dq_far,
    sq, kvs, kvr, dks, dkr, pr,
    qacc, kacc, vacc, dacc,
    load_sem, ga_s, ga_r, gg_s, gg_r, zm_s, zm_r, zd_s, zd_r, xo_s, xo_r, xq_s, xq_r,
    sm_s, sm_r, cp_s, cp_r,
):
    dp = lax.axis_index("dp")
    me = lax.axis_index("tensor")
    z, yh = me // 2, lax.rem(me, 2)
    x, yl, core = dp // 4, lax.rem(dp // 2, 2), lax.rem(dp, 2)
    sent = []

    def copy(src, dst, ssem, rsem, **where):
        return pltpu.make_async_remote_copy(
            src_ref=src, dst_ref=dst, send_sem=ssem, recv_sem=rsem,
            device_id=where, device_id_type=MESH,
        )

    def push(*args, **where):
        c = copy(*args, **where)
        c.start()
        sent.append(c)

    def zdev(sign):
        return lax.rem(z + sign + NZ, NZ) * 2 + yh

    def xdev(sign):
        return lax.rem(x + sign + NX, NX) * 4 + yl * 2 + core

    ypart = z * 2 + (1 - yh)
    ylpart = x * 4 + (1 - yl) * 2 + core
    cpart = x * 4 + yl * 2 + (1 - core)

    loads = [
        pltpu.make_async_copy(wk_hbm, wk, load_sem.at[0]),
        pltpu.make_async_copy(wv_hbm, wv, load_sem.at[1]),
        pltpu.make_async_copy(wq_hbm, wq, load_sem.at[2]),
        pltpu.make_async_copy(wo_hbm, wo, load_sem.at[3]),
    ]
    for c in loads:
        c.start()

    barrier = pltpu.get_barrier_semaphore()

    def greet(o, carry):
        pl.semaphore_signal(
            barrier, inc=1, device_id={"tensor": lax.rem(me + o, 16)}, device_id_type=MESH
        )
        return carry

    lax.fori_loop(1, 16, greet, 0)
    for d in (xdev(1), xdev(-1), ylpart, cpart):
        pl.semaphore_signal(barrier, inc=1, device_id={"dp": d}, device_id_type=MESH)

    lims = [E4_TOP * power_of_half(scale_ref[i]) for i in range(6)]
    glim = E5_TOP * power_of_half(scale_ref[6] + loss_ref[0])

    gout[z, yh] = clip(og_ref[0].astype(F32), glim).astype(BF)
    rows = tok_ref[0].astype(F32)

    def as_row(column):
        return jnp.broadcast_to(column, (TOK, 128)).T

    sq[me] = as_row(jnp.sum(rows * rows, axis=1, keepdims=True))[:8]
    pl.semaphore_wait(barrier, 19)

    def gather(buf, ss, rs):
        def view(zz, k, d, sign):
            v = buf.at[lax.rem(zz + NZ, NZ), yh if k == 0 else 1 - yh]
            if d == 4:
                v = v.at[pl.ds(0 if sign > 0 else TOK // 2, TOK // 2)]
            return v

        def number(d, k, sign):
            return 1 + (d - 1) * 4 + k * 2 + (0 if sign > 0 else 1)

        def side():
            push(buf.at[z, yh], buf.at[z, yh], ss.at[0], rs.at[0], tensor=ypart)

        def wait_side():
            v = buf.at[z, 1 - yh]
            copy(v, v, ss.at[0], rs.at[0], tensor=ypart).wait_recv()

        def send(d, k, sign):
            v = view(z - sign * (d - 1), k, d, sign)
            i = number(d, k, sign)
            push(v, v, ss.at[i], rs.at[i], tensor=zdev(sign))

        def wait(d, k, sign):
            v = view(z - sign * d, k, d, sign)
            i = number(d, k, sign)
            copy(v, v, ss.at[i], rs.at[i], tensor=zdev(sign)).wait_recv()

        return side, wait_side, send, wait

    def exchange(src, dst, j):
        def start(o, carry):
            peer = lax.rem(me + o, 16)
            copy(src(peer), dst.at[me], sm_s.at[j, o], sm_r.at[j, o], tensor=peer).start()
            return carry

        def recv(o, carry):
            origin = lax.rem(me + 16 - o, 16)
            copy(src(me), dst.at[origin], sm_s.at[j, o], sm_r.at[j, o], tensor=origin).wait_recv()
            return carry

        def drain(o, carry):
            peer = lax.rem(me + o, 16)
            copy(src(peer), dst.at[me], sm_s.at[j, o], sm_r.at[j, o], tensor=peer).wait_send()
            return carry

        return (
            lambda: lax.fori_loop(1, 16, start, 0),
            lambda: lax.fori_loop(1, 16, recv, 0),
            lambda: lax.fori_loop(1, 16, drain, 0),
        )

    sq_start, sq_wait, sq_drain = exchange(lambda peer: sq.at[me], sq, 0)
    kv_start, kv_wait, kv_drain = exchange(lambda peer: kvs.at[peer // 4], kvr, 1)
    dk_start, dk_wait, dk_drain = exchange(lambda peer: dks.at[peer], dkr, 2)
    pr_start, pr_wait, pr_drain = exchange(lambda peer: pr.at[me], pr, 3)

    sq_start()
    g_side, g_wait_side, g_send, g_wait = gather(gout, gg_s, gg_r)
    a_side, a_wait_side, a_send, a_wait = gather(acts, ga_s, ga_r)
    g_side()
    for sign in DIRS:
        g_send(1, 0, sign)

    pos = pos_ref[...]
    pair = lax.broadcasted_iota(jnp.int32, (64, TOK), 0).astype(F32)
    angle = pos.astype(F32) * jnp.exp(pair * (-2.0 * math.log(500000.0) / HD))
    cosine, sine = jnp.cos(angle), jnp.sin(angle)

    g_wait_side()
    for sign in DIRS:
        g_send(1, 1, sign)
    sq_wait()
    inv_row = lax.rsqrt(jnp.sum(sq[...], axis=0) / (FEAT * 16) + 1e-05)
    inv = jnp.broadcast_to(inv_row[:1], (128, TOK)).T[:, :1]
    gain = gain_ref[...]
    acts[z, yh] = clip(rows * inv * gain, lims[0]).astype(BF)
    a_side()
    for sign in DIRS:
        a_send(1, 0, sign)

    loads[0].wait()
    loads[1].wait()
    loads[2].wait()

    def trim_in(i, carry):
        r = pl.ds(pl.multiple_of(i * 512, 512), 512)
        wq[r, :] = clip(wq[r, :].astype(F32), lims[1]).astype(BF)
        wk[r, :] = clip(wk[r, :].astype(F32), lims[2]).astype(BF)
        wv[r, :] = clip(wv[r, :].astype(F32), lims[3]).astype(BF)
        return carry

    a_wait_side()
    for sign in DIRS:
        a_send(1, 1, sign)
    lax.fori_loop(0, 16, trim_in, 0)
    qacc[...] = jnp.zeros_like(qacc)
    kacc[...] = jnp.zeros_like(kacc)
    vacc[...] = jnp.zeros_like(vacc)
    dacc[...] = jnp.zeros_like(dacc)

    def project(zz, k):
        zs, ys = lax.rem(zz + NZ, NZ), (yh if k == 0 else 1 - yh)
        r = pl.ds(pl.multiple_of((zs * 2 + ys) * 512, 512), 512)
        a = acts[zs, ys]
        qacc[...] += nn(a, wq[r, :])
        kacc[...] += nn(a, wk[r, :])
        vacc[...] += nn(a, wv[r, :])

    def back(zz, k):
        zs, ys = lax.rem(zz + NZ, NZ), (yh if k == 0 else 1 - yh)
        r = pl.ds(pl.multiple_of((zs * 2 + ys) * 512, 512), 512)
        dacc[...] += nt(wo[:, r], gout[zs, ys])

    for k in (0, 1):
        project(z, k)
    for d in (1, 2, 3):
        for k in (0, 1):
            for sign in DIRS:
                a_wait(d, k, sign)
                a_send(d + 1, k, sign)
        if d == 3:
            for k in (0, 1):
                for sign in DIRS:
                    g_wait(1, k, sign)
                    g_send(2, k, sign)
        for k in (0, 1):
            for sign in DIRS:
                project(z - sign * d, k)

    loads[3].wait()

    def trim_out(i, carry):
        r = pl.ds(pl.multiple_of(i * 512, 512), 512)
        wo[:, r] = clip(wo[:, r].astype(F32), lims[4]).astype(BF)
        return carry

    lax.fori_loop(0, 16, trim_out, 0)
    for k in (0, 1):
        for sign in DIRS:
            a_wait(4, k, sign)
        project(z + 4, k)
    push(acts.at[:, 1 - core], pacts, cp_s.at[0], cp_r.at[0], dp=cpart)

    o64 = lax.broadcasted_iota(jnp.int32, (64, KC), 0)
    c64 = lax.broadcasted_iota(jnp.int32, (64, KC), 1)
    wanted = (o64 & 7) * 4 + (o64 >> 4)
    is_value = ((o64 >> 3) & 1) == 1
    hit = c64 == wanted
    pick_k = jnp.where(hit & jnp.logical_not(is_value), 1.0, 0.0).astype(BF)
    pick_v = jnp.where(hit & is_value, 1.0, 0.0).astype(BF)
    kv_rows = nt(pick_k, kacc[...].astype(BF)) + nt(pick_v, vacc[...].astype(BF))
    kvs[...] = kv_rows.astype(BF).reshape(4, 16, TOK)
    kv_start()
    kvr[me] = kvs[me // 4]

    q_t = qacc[...].astype(BF).astype(F32).T
    q_rot = [rot(q_t[h * HD : (h + 1) * HD], cosine, sine) for h in range(2)]
    for k in (0, 1):
        for sign in DIRS:
            g_wait(2, k, sign)
            g_send(3, k, sign)
    for d in (1, 2):
        for k in (0, 1):
            for sign in DIRS:
                back(z - sign * d, k)

    kv_wait()
    kv = kvr[...].astype(F32)
    k_t = kv[:, :8].reshape(HD, TOK)
    v_t = kv[:, 8:].reshape(HD, TOK)
    k_rot = rot(k_t, cosine, sine)
    k_rows = k_rot.T
    v_t16 = v_t.astype(BF)
    v_rows = v_t.T.astype(BF)
    src = lax.broadcasted_iota(jnp.int32, (TOK, TOK), 0)
    dst = lax.broadcasted_iota(jnp.int32, (TOK, TOK), 1)
    allowed = (src <= dst) & (src >= dst - pos)
    probs = []
    for h in range(2):
        score = precise(nn, k_rows, q_rot[h]) * (1.0 / math.sqrt(HD))
        weight = jnp.where(allowed, jnp.exp(jnp.where(allowed, score, 0.0)), 0.0)
        p = weight / jnp.sum(weight, axis=0, keepdims=True)
        probs.append(p)
        att = nn(v_t16, p.astype(BF)).astype(BF).astype(F32)
        att_own[pl.ds(h * HD, HD), :] = clip(att, lims[5]).astype(BF)
    push(att_own, att_far, cp_s.at[1], cp_r.at[1], dp=cpart)
    att_rows = att_own[...].astype(F32).T.astype(BF)
    for k in (0, 1):
        for sign in DIRS:
            g_wait(3, k, sign)
            g_send(4, k, sign)

    def scatter(p, r, y, ss, rs):
        rows_n = p.shape[2]
        half = rows_n // 2

        def part(v, sign):
            return v.at[pl.ds(0 if sign > 0 else half, half)]

        def number(st, k, sign):
            return (st - 1) * 4 + k * 2 + (0 if sign > 0 else 1)

        def where(zz, k):
            return lax.rem(zz + NZ, NZ), (yh if k == 0 else 1 - yh)

        def ends(st, k, sign):
            to = r.at[0 if sign > 0 else 1, st - 1, k]
            return part(to, sign) if st == 1 else to

        def send(st, k, sign):
            zs, ys = where(z + sign * (5 - st), k)
            v = p.at[zs, ys]
            if st == 1:
                v = part(v, sign)
            i = number(st, k, sign)
            push(v, ends(st, k, sign), ss.at[i], rs.at[i], tensor=zdev(sign))

        def wait(st, k, sign):
            v = ends(st, k, sign)
            i = number(st, k, sign)
            copy(v, v, ss.at[i], rs.at[i], tensor=zdev(sign)).wait_recv()

        def step(st, k, sign):
            wait(st, k, sign)
            zs, ys = where(z + sign * (4 - st), k)
            j = 0 if sign > 0 else 1
            if st == 1:
                a = pl.ds(0 if sign > 0 else half, half)
            else:
                a = pl.ds(0, rows_n)
            p[zs, ys, a] = (p[zs, ys, a].astype(F32) + r[j, st - 1, k, a].astype(F32)).astype(BF)
            send(st + 1, k, sign)

        def total(k):
            for sign in DIRS:
                wait(4, k, sign)
            ys = yh if k == 0 else 1 - yh
            return p[z, ys].astype(F32) + (r[0, 3, k].astype(F32) + r[1, 3, k].astype(F32))

        def cross():
            p[z, 1 - yh] = total(1).astype(BF)
            push(p.at[z, 1 - yh], y, ss.at[16], rs.at[16], tensor=ypart)

        def finish():
            own = total(0)
            copy(y, y, ss.at[16], rs.at[16], tensor=ypart).wait_recv()
            return own + y[...].astype(F32)

        return send, step, cross, finish

    def group_sum(p, r, y, ss, rs):
        rows_n = p.shape[1]
        half = rows_n // 2

        def where(xx, k):
            return lax.rem(xx + NX, NX) * 2 + (yl if k == 0 else 1 - yl)

        def number(st, k, sign):
            return (st - 1) * 4 + k * 2 + (0 if sign > 0 else 1)

        def ends(st, k, sign):
            to = r.at[0 if sign > 0 else 1, st - 1, k]
            return to.at[pl.ds(0 if sign > 0 else half, half)] if st == 1 else to

        def send(st, k, sign):
            v = p.at[where(x + sign * (3 - st), k)]
            if st == 1:
                v = v.at[pl.ds(0 if sign > 0 else half, half)]
            i = number(st, k, sign)
            push(v, ends(st, k, sign), ss.at[i], rs.at[i], dp=xdev(sign))

        def wait(st, k, sign):
            v = ends(st, k, sign)
            i = number(st, k, sign)
            copy(v, v, ss.at[i], rs.at[i], dp=xdev(sign)).wait_recv()

        def step(k, sign):
            wait(1, k, sign)
            s = where(x + sign, k)
            a = pl.ds(0 if sign > 0 else half, half)
            j = 0 if sign > 0 else 1
            p[s, a] = (p[s, a].astype(F32) + r[j, 0, k, a].astype(F32)).astype(BF)
            send(2, k, sign)

        def total(k):
            for sign in DIRS:
                wait(2, k, sign)
            return p[where(x, k)].astype(F32) + (r[0, 1, k].astype(F32) + r[1, 1, k].astype(F32))

        def cross():
            p[where(x, 1)] = total(1).astype(BF)
            push(p.at[where(x, 1)], y, ss.at[8], rs.at[8], dp=ylpart)

        def finish():
            own = total(0)
            copy(y, y, ss.at[8], rs.at[8], dp=ylpart).wait_recv()
            return own + y[...].astype(F32)

        return send, step, cross, finish

    m_send, m_step, m_cross, m_finish = scatter(pm, rm, ym, zm_s, zm_r)
    n_send, n_step, n_cross, n_finish = scatter(pd, rd, yd, zd_s, zd_r)
    o_send, o_step, o_cross, o_finish = group_sum(sgo, xgo, ygo, xo_s, xo_r)
    w_send, w_step, w_cross, w_finish = group_sum(sgq, xgq, ygq, xq_s, xq_r)
    K_ORDER = (1, 0)

    def mix(i, carry):
        zs, ys = lax.rem(z + 4 + i // 2, NZ), lax.rem(i, 2)
        r = pl.ds(pl.multiple_of((zs * 2 + ys) * 512, 512), 512)
        pm[zs, ys] = nn(att_rows, wo[:, r]).astype(BF)
        return carry

    lax.fori_loop(0, 2, mix, 0)
    for k in K_ORDER:
        for sign in DIRS:
            m_send(1, k, sign)
    lax.fori_loop(2, 16, mix, 0)

    for k in (0, 1):
        for sign in DIRS:
            g_wait(4, k, sign)
    push(gout.at[:, 1 - core], pgout, cp_s.at[2], cp_r.at[2], dp=cpart)
    for k in (0, 1):
        for sign in DIRS:
            m_step(1, 1 - k, sign)
    for k in (0, 1):
        back(z, k)
        back(z + 4, k)
        for sign in DIRS:
            back(z - sign * 3, k)

    d_t = dacc[...].astype(BF)
    dk_rot = jnp.zeros((HD, TOK), F32)
    dv_t = jnp.zeros((HD, TOK), F32)
    for h in range(2):
        g = d_t[h * HD : (h + 1) * HD]
        p = probs[h]
        dw = nn(v_rows, g)
        delta = jnp.sum(p * dw, axis=0, keepdims=True)
        ds = p * (dw - delta) * (1.0 / math.sqrt(HD))
        p_high, p_low = halves(p)
        dv_t = dv_t + nt(g, p_high) + nt(g, p_low)
        dq_own[pl.ds(h * HD, HD), :] = unrot(precise(nn, k_rot, ds), cosine, sine).astype(BF)
        dk_rot = dk_rot + precise(nt, q_rot[h], ds)
    dk_t = unrot(dk_rot, cosine, sine)
    dks[...] = jnp.concatenate(
        [dk_t.reshape(16, 8, TOK), dv_t.reshape(16, 8, TOK)], axis=1
    ).astype(BF)
    dk_start()
    dkr[me] = dks[me]

    copy(gout.at[:, core], pgout, cp_s.at[2], cp_r.at[2], dp=cpart).wait_recv()
    copy(att_own, att_far, cp_s.at[1], cp_r.at[1], dp=cpart).wait_recv()

    def out_grads(i, carry):
        s = lax.rem(2 * x + 4 + i, 8)
        sgo[s] = (nn(att_own[...], gout[s, core]) + nn(att_far[...], pgout[s])).astype(BF)
        return carry

    lax.fori_loop(0, 2, out_grads, 0)
    for k in K_ORDER:
        for sign in DIRS:
            o_send(1, k, sign)
    lax.fori_loop(2, 8, out_grads, 0)
    for k in K_ORDER:
        for sign in DIRS:
            m_step(2, k, sign)

    dk_wait()
    o4 = lax.broadcasted_iota(jnp.int32, (64, 64), 0)
    i4 = lax.broadcasted_iota(jnp.int32, (64, 64), 1)
    low = o4 & 31
    pick = jnp.where(i4 == (low & 3) * 16 + (o4 >> 5) * 8 + (low >> 2), 1.0, 0.0).astype(BF)
    dkv = jnp.sum(dkr[...].astype(F32).reshape(4, 4, 16, TOK), axis=1).reshape(64, TOK)
    dq_own[pl.ds(QC, 64), :] = nn(pick, dkv.astype(BF)).astype(BF)
    push(dq_own, dq_far, cp_s.at[3], cp_r.at[3], dp=cpart)

    def down(i, carry):
        zs, ys = lax.rem(z + 4 + i // 2, NZ), lax.rem(i, 2)
        r = pl.ds(pl.multiple_of((zs * 2 + ys) * 512, 512), 512)
        term = nn(wq[r, :], dq_own[pl.ds(0, QC), :])
        term = term + nn(wk[r, :], dq_own[pl.ds(QC, KC), :])
        term = term + nn(wv[r, :], dq_own[pl.ds(QC + KC, KC), :])
        pd[zs, ys] = term.astype(BF)
        return carry

    lax.fori_loop(0, 2, down, 0)
    for k in K_ORDER:
        for sign in DIRS:
            m_step(3, k, sign)
    for k in K_ORDER:
        for sign in DIRS:
            n_send(1, k, sign)
    lax.fori_loop(2, 16, down, 0)
    for k in K_ORDER:
        for sign in DIRS:
            o_step(k, sign)

    copy(acts.at[:, core], pacts, cp_s.at[0], cp_r.at[0], dp=cpart).wait_recv()
    copy(dq_own, dq_far, cp_s.at[3], cp_r.at[3], dp=cpart).wait_recv()

    def in_grads(i, carry):
        s = lax.rem(2 * x + 4 + i, 8)
        sgq[s] = (nn(dq_own[...], acts[s, core]) + nn(dq_far[...], pacts[s])).astype(BF)
        return carry

    lax.fori_loop(0, 2, in_grads, 0)
    for k in K_ORDER:
        for sign in DIRS:
            w_send(1, k, sign)
    lax.fori_loop(2, 8, in_grads, 0)

    for k in K_ORDER:
        for sign in DIRS:
            n_step(1, k, sign)
    m_cross()
    for k in K_ORDER:
        for sign in DIRS:
            n_step(2, k, sign)
    mixed_ref[0] = m_finish().astype(BF)
    o_cross()
    for k in K_ORDER:
        for sign in DIRS:
            w_step(k, sign)
    for k in K_ORDER:
        for sign in DIRS:
            n_step(3, k, sign)
    go_ref[...] = o_finish()
    n_cross()
    w_cross()
    scaled = n_finish().T * gain
    pr[me] = as_row(jnp.sum(rows * scaled, axis=1, keepdims=True))[:8]
    pr_start()
    gqkv_ref[...] = w_finish()
    pr_wait()
    proj = jnp.broadcast_to(jnp.sum(pr[...], axis=0)[:1], (128, TOK)).T[:, :1]
    slope = inv * inv * inv * proj / (FEAT * 16)
    dtok_ref[0] = (inv * scaled - rows * slope).astype(BF)

    for c in sent:
        c.wait_send()
    sq_drain()
    kv_drain()
    dk_drain()
    pr_drain()


def body(
    tokens, norm_gain, w_query, w_key, w_value, w_output, positions, scale_exps, loss_exp, out_grad
):
    vmem = pl.BlockSpec(memory_space=pltpu.VMEM)
    smem = pl.BlockSpec(memory_space=pltpu.SMEM)
    hbm = pl.BlockSpec(memory_space=pl.ANY)
    V = pltpu.VMEM
    dma = pltpu.SemaphoreType.DMA
    mixed, d_rows, gqkv, grad_output = pl.pallas_call(
        kernel,
        out_shape=(
            jax.ShapeDtypeStruct((1, TOK, FEAT), BF),
            jax.ShapeDtypeStruct((1, TOK, FEAT), BF),
            jax.ShapeDtypeStruct((QC + 2 * KC, FEAT), F32),
            jax.ShapeDtypeStruct((QC, FEAT), F32),
        ),
        in_specs=[smem, smem, vmem, vmem, vmem, vmem, hbm, hbm, hbm, hbm],
        out_specs=(vmem, vmem, vmem, vmem),
        scratch_shapes=[
            V((8192, QC), BF), V((8192, KC), BF), V((8192, KC), BF), V((QC, 8192), BF),
            V((8, 2, TOK, FEAT), BF), V((8, 2, TOK, FEAT), BF),
            V((8, TOK, FEAT), BF), V((8, TOK, FEAT), BF),
            V((8, 2, TOK, FEAT), BF), V((2, 4, 2, TOK, FEAT), BF), V((TOK, FEAT), BF),
            V((8, 2, FEAT, TOK), BF), V((2, 4, 2, FEAT, TOK), BF), V((FEAT, TOK), BF),
            V((8, QC, FEAT), BF), V((2, 2, 2, QC, FEAT), BF), V((QC, FEAT), BF),
            V((8, QC + 64, FEAT), BF), V((2, 2, 2, QC + 64, FEAT), BF), V((QC + 64, FEAT), BF),
            V((QC, TOK), BF), V((QC, TOK), BF), V((QC + 64, TOK), BF), V((QC + 64, TOK), BF),
            V((16, 8, TOK), F32), V((4, 16, TOK), BF), V((16, 16, TOK), BF),
            V((16, 16, TOK), BF), V((16, 16, TOK), BF), V((16, 8, TOK), F32),
            V((TOK, QC), F32), V((TOK, KC), F32), V((TOK, KC), F32), V((QC, TOK), F32),
            dma((4,)), dma((17,)), dma((17,)), dma((17,)), dma((17,)),
            dma((17,)), dma((17,)), dma((17,)), dma((17,)),
            dma((9,)), dma((9,)), dma((9,)), dma((9,)),
            dma((4, 16)), dma((4, 16)), dma((4,)), dma((4,)),
        ],
        compiler_params=pltpu.CompilerParams(
            collective_id=0, has_side_effects=True, vmem_limit_bytes=60 * 1024 * 1024
        ),
    )(
        scale_exps, loss_exp, tokens, norm_gain.astype(F32)[None], positions, out_grad,
        w_query, w_key, w_value, w_output,
    )
    grad_query = gqkv[:QC].T
    grad_key = gqkv[QC : QC + KC].T
    grad_value = gqkv[QC + KC :].T
    return mixed, d_rows, grad_query, grad_key, grad_value, grad_output


def solution(mesh):
    placed = (
        P("dp", None, "tensor"),
        P("tensor"),
        P(None, "tensor"),
        P(None, "tensor"),
        P(None, "tensor"),
        P("tensor", None),
        P("dp", None),
        P(),
        P(),
        P("dp", None, "tensor"),
    )
    return jax.shard_map(
        body,
        mesh=mesh,
        in_specs=placed,
        out_specs=(
            P("dp", None, "tensor"),
            P("dp", None, "tensor"),
            P("dp", "tensor"),
            P("dp", "tensor"),
            P("dp", "tensor"),
            P("tensor", "dp"),
        ),
        check_vma=False,
    )
```

```python
import functools
import math

import jax
import jax.numpy as jnp
from jax import lax
from jax.experimental import pallas as pl
from jax.experimental.pallas import tpu as pltpu
from jax.sharding import PartitionSpec as P

HD = 128
E4_TOP = 448.0
E5_TOP = 57344.0
BF = jnp.bfloat16
F32 = jnp.float32
MESH = pl.DeviceIdType.MESH
NZ, NX, TOK, FEAT, QC, KC = 8, 4, 128, 512, 256, 32
DIRS = (1, -1)


def nn(a, b):
    return jnp.dot(a, b, preferred_element_type=F32)


def nt(a, b):
    return lax.dot_general(a, b, (((1,), (1,)), ((), ())), preferred_element_type=F32)


def halves(a):
    high = a.astype(BF)
    return high, (a - high.astype(F32)).astype(BF)


def precise(dot, a, b):
    ah, al = halves(a)
    bh, bl = halves(b)
    return dot(ah, bh) + (dot(ah, bl) + dot(al, bh))


def power_of_half(e):
    out = jnp.float32(1.0)
    for bit in range(5):
        out = out * jnp.where(((e >> bit) & 1) == 1, jnp.float32(2.0 ** -(1 << bit)), jnp.float32(1.0))
    return out


def clip(v, limit):
    return jnp.minimum(jnp.maximum(v, -limit), limit)


def rot(v, c, s):
    return jnp.concatenate([v[:64] * c - v[64:] * s, v[64:] * c + v[:64] * s], axis=0)


def unrot(v, c, s):
    return jnp.concatenate([v[:64] * c + v[64:] * s, v[64:] * c - v[:64] * s], axis=0)


ORDER = (
    0, 16, 32, 2, 9, 1, 33, 78, 108, 58, 113, 98, 68, 73, 93, 48, 43, 118, 83, 63, 44, 88, 53, 103,
    52, 3, 10, 13, 62, 47, 6, 57, 82, 42, 18, 25, 17, 49, 84, 54, 12, 92, 5, 87, 4, 7, 67, 11, 72,
    14, 19, 26, 64, 59, 22, 29, 21, 28, 94, 89, 97, 102, 107, 8, 15, 77, 112, 20, 27, 23, 69, 30,
    74, 99, 104, 117, 34, 24, 35, 31, 79, 38, 109, 114, 119, 37, 36, 80, 120, 123, 39, 115, 132,
    75, 110, 126, 160, 164, 70, 100, 127, 105, 133, 40, 65, 60, 155, 90, 161, 153, 157, 95, 162,
    156, 124, 163, 154, 55, 171, 177, 175, 179, 128, 45, 134, 85, 169, 166, 165, 50, 41, 121, 138,
    81, 116, 51, 147, 111, 141, 135, 76, 129, 159, 158, 91, 106, 148, 71, 46, 86, 66, 56, 96, 61,
    101, 142, 125, 122, 183, 187, 181, 185, 186, 139, 136, 192, 193, 130, 191, 178, 170, 149, 176,
    143, 180, 167, 168, 184, 190, 194, 172, 150, 144, 131, 137, 188, 189, 140, 199, 151, 145, 182,
    196, 195, 198, 174, 173, 152, 146, 197, 201, 202, 203, 200,
)


def kernel(
    scale_ref, loss_ref, tok_ref, gain_ref, pos_ref, og_ref, wq_hbm, wk_hbm, wv_hbm, wo_hbm,
    mixed_hbm, dtok_hbm, gq_hbm, gkv_hbm, go_hbm,
    mixed_out, dtok_out, gq_out, go_out, gkv_out,
    wq, wkt, wvt, wkv, wo, toks, acts, gout, pacts, pgout,
    pm, rm0, rm1, ym, pd, rd0, rd1, yd,
    sgo, xgo, ygo, sgw, xgw, ygw, sgv, xgv, ygv,
    att_own, att_far, dq_own, dq_far, dk_own, dk_far, probs, q_rot, k_rot, v_rows, lane_inv,
    angles, projected, scaled_rows,
    mg, kvs, kvr, dks, dkr, pr,
    qacc, kvacc, dacc,
    load_sem, out_sem, gt_s, gt_r, gg_s, gg_r, zm_s, zm_r, zd_s, zd_r, xo_s, xo_r,
    xw_s, xw_r, xv_s, xv_r, sm_s, sm_r, cp_s, cp_r,
):
    dp = lax.axis_index("dp")
    me = lax.axis_index("tensor")
    z, yh = me // 2, lax.rem(me, 2)
    x, yl, core = dp // 4, lax.rem(dp // 2, 2), lax.rem(dp, 2)
    sent = []
    tasks = {}
    K_ORDER = (1, 0)
    SLOTS = [(d, k, g) for k in (0, 1) for d in range(5) for g in (DIRS if 0 < d < 4 else (1,))]

    def name(head, *parts):
        return head + ",".join(("+" if v > 0 else "-") if n == len(parts) - 1 else str(v) for n, v in enumerate(parts))

    def task(key, *steps):
        tasks[key] = steps

    def call(f, *args):
        return functools.partial(f, *args)

    def copy(src, dst, ssem, rsem, **where):
        return pltpu.make_async_remote_copy(
            src_ref=src, dst_ref=dst, send_sem=ssem, recv_sem=rsem,
            device_id=where, device_id_type=MESH,
        )

    def push(*args, **where):
        c = copy(*args, **where)
        c.start()
        sent.append(c)

    def zdev(sign):
        return lax.rem(z + sign + NZ, NZ) * 2 + yh

    def xdev(sign):
        return lax.rem(x + sign + NX, NX) * 4 + yl * 2 + core

    ypart = z * 2 + (1 - yh)
    ylpart = x * 4 + (1 - yl) * 2 + core
    cpart = x * 4 + yl * 2 + (1 - core)

    loads = [
        pltpu.make_async_copy(wk_hbm, wkt, load_sem.at[0]),
        pltpu.make_async_copy(wv_hbm, wvt, load_sem.at[1]),
        pltpu.make_async_copy(wq_hbm, wq, load_sem.at[2]),
        pltpu.make_async_copy(wo_hbm, wo, load_sem.at[3]),
    ]
    for c in loads:
        c.start()

    barrier = pltpu.get_barrier_semaphore()

    def greet(o, carry):
        pl.semaphore_signal(
            barrier, inc=1, device_id={"tensor": lax.rem(me + o, 16)}, device_id_type=MESH
        )
        return carry

    lax.fori_loop(1, 16, greet, 0)
    for other in (xdev(1), xdev(-1), ylpart, cpart):
        pl.semaphore_signal(barrier, inc=1, device_id={"dp": other}, device_id_type=MESH)

    lims = [E4_TOP * power_of_half(scale_ref[i]) for i in range(6)]
    glim = E5_TOP * power_of_half(scale_ref[6] + loss_ref[0])

    toks[z, yh] = tok_ref[0]
    gout[z, yh] = clip(og_ref[0].astype(F32), glim).astype(BF)
    rows = tok_ref[0].astype(F32)
    gain = gain_ref[...].astype(F32).reshape(1, FEAT)

    def as_row(column):
        return jnp.broadcast_to(column, (TOK, 128)).T

    lanes = [gain[:, i * 128 : (i + 1) * 128] for i in range(4)]
    squares_own = as_row(jnp.sum(rows * rows, axis=1, keepdims=True))[:4]
    mg[me] = jnp.concatenate(lanes + [squares_own], axis=0)
    pos = pos_ref[...]
    pair = lax.broadcasted_iota(jnp.int32, (64, TOK), 0).astype(F32)
    angle = pos.astype(F32) * jnp.exp(pair * (-2.0 * math.log(500000.0) / HD))
    angles[0] = jnp.cos(angle)
    angles[1] = jnp.sin(angle)
    qacc[...] = jnp.zeros_like(qacc)
    kvacc[...] = jnp.zeros_like(kvacc)
    dacc[...] = jnp.zeros_like(dacc)
    projected[...] = jnp.zeros_like(projected)
    pl.semaphore_wait(barrier, 19)

    def spot(zz, k):
        return lax.rem(zz + NZ, NZ), (yh if k == 0 else 1 - yh)

    def half_of(sign):
        return pl.ds(0 if sign > 0 else TOK // 2, TOK // 2)

    def gather(p, buf, ss, rs):
        def view(zz, k, part=None):
            zs, ys = spot(zz, k)
            return buf.at[zs, ys] if part is None else buf.at[zs, ys, half_of(part)]

        def ring(d, k, sign, zz):
            cut = sign if (d == 4 or (d == 2 and k == 1)) else None
            i = (d - 1) * 2 + (0 if sign > 0 else 1) + 8 * k
            return view(zz, k, cut), i

        def send(d, k, sign):
            v, i = ring(d, k, sign, z - sign * (d - 1))
            push(v, v, ss.at[i], rs.at[i], tensor=zdev(sign))

        def wait(d, k, sign):
            v, i = ring(d, k, sign, z - sign * d)
            copy(v, v, ss.at[i], rs.at[i], tensor=zdev(sign)).wait_recv()

        def side(d, k, sign):
            i = 12 + d * 2 + (0 if sign > 0 else 1)
            cut = {0: None, 2: -sign, 3: None, 4: sign}[d]
            return view(z - sign * d, k, cut), i

        def send_side(d, sign):
            v, i = side(d, 0, sign)
            push(v, v, ss.at[i], rs.at[i], tensor=ypart)

        def wait_side(d, sign):
            v, i = side(d, 1, sign)
            copy(v, v, ss.at[i], rs.at[i], tensor=ypart).wait_recv()

        def begin():
            send_side(0, 1)
            for g in DIRS:
                send(1, 0, g)

        def partner():
            wait_side(0, 1)
            for g in DIRS:
                send(1, 1, g)

        task(p + "0", begin)
        task(p + "f1,1", partner)
        for g in DIRS:
            for d, k in ((2, 0), (3, 0), (4, 0), (2, 1)):
                task(name(p + "f", d, k, g), call(wait, d - 1, k, g), call(send, d, k, g))
            task(name(p + "s2,", g), call(send_side, 2, g))
            task(name(p + "s3,", g), call(send_side, 3, g))
            task(name(p + "s4,", g), call(wait, 4, 0, g), call(send_side, 4, g))

        def arrived(d, k, g):
            if k == 1 and d > 0:
                if d == 1:
                    return
                if d == 2:
                    wait(2, 1, g)
                for h in DIRS if d == 4 else (g,):
                    wait_side(d, h)

        return arrived

    def exchange(src, dst, j):
        def start(o, carry):
            peer = lax.rem(me + o, 16)
            copy(src(peer), dst.at[me], sm_s.at[j, o], sm_r.at[j, o], tensor=peer).start()
            return carry

        def recv(o, carry):
            origin = lax.rem(me + 16 - o, 16)
            copy(src(me), dst.at[origin], sm_s.at[j, o], sm_r.at[j, o], tensor=origin).wait_recv()
            return carry

        def drain(o, carry):
            peer = lax.rem(me + o, 16)
            copy(src(peer), dst.at[me], sm_s.at[j, o], sm_r.at[j, o], tensor=peer).wait_send()
            return carry

        return (
            lambda: lax.fori_loop(1, 16, start, 0),
            lambda: lax.fori_loop(1, 16, recv, 0),
            lambda: lax.fori_loop(1, 16, drain, 0),
        )

    mg_start, mg_wait, mg_drain = exchange(lambda peer: mg.at[me], mg, 0)
    kv_start, kv_wait, kv_drain = exchange(lambda peer: kvs.at[peer // 4], kvr, 1)
    dk_start, dk_wait, dk_drain = exchange(lambda peer: dks.at[peer], dkr, 2)
    pr_start, pr_wait, pr_drain = exchange(lambda peer: pr.at[me], pr, 3)

    t_arrived = gather("T", toks, gt_s, gt_r)
    g_arrived = gather("G", gout, gg_s, gg_r)
    task("mg", mg_start)

    def gain_of(slot):
        g = mg[slot]
        return jnp.concatenate([g[i : i + 1] for i in range(4)], axis=1)

    def prepare():
        mg_wait()
        squares = jnp.sum(mg[...], axis=0)[4:5]
        inv_row = lax.rsqrt(squares / (FEAT * 16) + 1e-05)
        lane_inv[...] = jnp.broadcast_to(inv_row[:1], (128, TOK)).T
        for c in loads:
            c.wait()

    task("pre", prepare)

    def block(d, k, g):
        zs, ys = spot(z - g * d, k)
        return zs, ys, pl.ds(pl.multiple_of((zs * 2 + ys) * 512, 512), 512)

    def project(d, k, g):
        t_arrived(d, k, g)
        zs, ys, r = block(d, k, g)
        inv = lane_inv[:, pl.ds(0, 1)]
        a = toks[zs, ys].astype(F32) * inv * gain_of(zs * 2 + ys)
        a = clip(a, lims[0]).astype(BF)
        acts[zs, ys] = a
        w = clip(wq[r, :].astype(F32), lims[1]).astype(BF)
        wq[r, :] = w
        wn = jnp.concatenate(
            [clip(wkt[:, r].astype(F32), lims[2]), clip(wvt[:, r].astype(F32), lims[3])], axis=0
        ).T.astype(BF)
        wkv[r, :] = wn
        qacc[...] += nn(a, w)
        kvacc[...] += nn(a, wn)

    def cast_out(d, k, g):
        zs, ys, r = block(d, k, g)
        wo[:, r] = clip(wo[:, r].astype(F32), lims[4]).astype(BF)

    def back(d, k, g):
        g_arrived(d, k, g)
        zs, ys, r = block(d, k, g)
        dacc[...] += nt(wo[:, r], gout[zs, ys])

    def natural(i):
        low = i & 31
        return (low & 3) * 16 + (i >> 5) * 8 + (low >> 2)

    i0 = lax.broadcasted_iota(jnp.int32, (64, 64), 0)
    i1 = lax.broadcasted_iota(jnp.int32, (64, 64), 1)

    def send_kv():
        by_head = jnp.where(natural(i1) == i0, 1.0, 0.0).astype(BF)
        kvs[...] = nt(by_head, kvacc[...].astype(BF)).astype(BF).reshape(4, 16, TOK)
        kv_start()
        kvr[me] = kvs[me // 4]

    task("kv", send_kv)

    def turn_query():
        q_t = qacc[...].astype(BF).astype(F32).T
        for h in range(2):
            q_rot[h] = rot(q_t[h * HD : (h + 1) * HD], angles[0], angles[1])

    task("qrot", turn_query)

    def attend():
        kv_wait()
        kv = kvr[...].astype(F32)
        k_t = kv[:, :8].reshape(HD, TOK)
        v_t = kv[:, 8:].reshape(HD, TOK)
        k_turned = rot(k_t, angles[0], angles[1])
        k_rot[...] = k_turned
        k_rows = k_turned.T
        v_t16 = v_t.astype(BF)
        v_rows[...] = v_t.T.astype(BF)
        src = lax.broadcasted_iota(jnp.int32, (TOK, TOK), 0)
        dst = lax.broadcasted_iota(jnp.int32, (TOK, TOK), 1)
        allowed = (src <= dst) & (src >= dst - pos)
        for h in range(2):
            score = precise(nn, k_rows, q_rot[h]) * (1.0 / math.sqrt(HD))
            weight = jnp.where(allowed, jnp.exp(jnp.where(allowed, score, 0.0)), 0.0)
            p = weight / jnp.sum(weight, axis=0, keepdims=True)
            probs[h] = p
            att = nn(v_t16, p.astype(BF)).astype(BF).astype(F32)
            att_own[pl.ds(h * HD, HD), :] = clip(att, lims[5]).astype(BF)
        push(att_own, att_far, cp_s.at[1], cp_r.at[1], dp=cpart)

    task("att", attend)

    def mix(d, k, g):
        zs, ys, r = block(d, k, -g)
        att_rows = att_own[...].astype(F32).T.astype(BF)
        pm[zs, ys] = nn(att_rows, wo[:, r]).astype(BF)

    def share_gout():
        push(gout.at[:, 1 - core], pgout, cp_s.at[2], cp_r.at[2], dp=cpart)

    def share_acts():
        push(acts.at[:, 1 - core], pacts, cp_s.at[0], cp_r.at[0], dp=cpart)

    task("gpush", share_gout)
    task("apush", share_acts)

    def score_grad(h):
        g = dacc[pl.ds(h * HD, HD), :].astype(BF)
        dw = nn(v_rows[...], g)
        p = probs[h]
        delta = jnp.sum(p * dw, axis=0, keepdims=True)
        return g, p, p * (dw - delta) * (1.0 / math.sqrt(HD))

    def backward():
        dk_rot = jnp.zeros((HD, TOK), F32)
        dv_t = jnp.zeros((HD, TOK), F32)
        for h in range(2):
            g, p, ds = score_grad(h)
            p_high, p_low = halves(p)
            dv_t = dv_t + nt(g, p_high) + nt(g, p_low)
            dk_rot = dk_rot + precise(nt, q_rot[h], ds)
            probs[h] = ds
        dk_t = unrot(dk_rot, angles[0], angles[1])
        dks[...] = jnp.concatenate(
            [dk_t.reshape(16, 8, TOK), dv_t.reshape(16, 8, TOK)], axis=1
        ).astype(BF)
        dk_start()
        dkr[me] = dks[me]

    task("bwd", backward)

    def query_grad():
        for h in range(2):
            dq = unrot(precise(nn, k_rot[...], probs[h]), angles[0], angles[1])
            dq_own[pl.ds(h * HD, HD), :] = dq.astype(BF)
        push(dq_own, dq_far, cp_s.at[3], cp_r.at[3], dp=cpart)

    task("bwq", query_grad)

    def key_grad():
        dk_wait()
        by_column = jnp.where(natural(i0) == i1, 1.0, 0.0).astype(BF)
        dkv = jnp.sum(dkr[...].astype(F32).reshape(4, 4, 16, TOK), axis=1).reshape(64, TOK)
        dk_own[...] = nn(by_column, dkv.astype(BF)).astype(BF)
        push(dk_own, dk_far, cp_s.at[4], cp_r.at[4], dp=cpart)

    task("dkfin", key_grad)

    def down(d, k, g):
        zs, ys, r = block(d, k, -g)
        term = (nn(wq[r, :], dq_own[...]) + nn(wkv[r, :], dk_own[...])).astype(BF)
        pd[zs, ys] = term
        high, low = halves(toks[zs, ys].astype(F32) * gain_of(zs * 2 + ys))
        projected[...] += nn(high, term) + nn(low, term)

    for d, k, g in SLOTS:
        task(name("proj", d, k, g), call(project, d, k, g))
        task(name("clipo", d, k, g), call(cast_out, d, k, g))
        task(name("back", d, k, g), call(back, d, k, g))
        task(name("mix", d, k, g), call(mix, d, k, g))
        task(name("down", d, k, g), call(down, d, k, g))

    def send_product():
        diagonal = lax.broadcasted_iota(jnp.int32, (TOK, TOK), 0) == lax.broadcasted_iota(
            jnp.int32, (TOK, TOK), 1
        )
        own = jnp.sum(jnp.where(diagonal, projected[...], 0.0), axis=0, keepdims=True)
        pr[me] = jnp.broadcast_to(own, (8, TOK))
        pr_start()

    task("prx", send_product)

    def scatter(q, p, r0, r1, y, ss, rs):
        rows_n = p.shape[2]
        half = rows_n // 2

        def cut(sign):
            return pl.ds(0 if sign > 0 else half, half)

        whole = pl.ds(0, rows_n)

        def place(d, k, sign):
            return spot(z + sign * d, k)

        def side_area(d, sign):
            return cut(-sign) if d == 2 else whole

        def side_slot(d, sign):
            return {4: 0, 3: 1, 2: 3, 0: 5}[d] + (1 if sign < 0 else 0)

        def send_side(d, sign=1):
            zs, ys = place(d, 1, sign)
            a, i = side_area(d, sign), side_slot(d, sign)
            push(p.at[zs, ys, a], y.at[i, a], ss.at[i], rs.at[i], tensor=ypart)

        def side(d, sign=1):
            a, i = side_area(d, sign), side_slot(d, sign)
            v = y.at[i, a]
            copy(v, v, ss.at[i], rs.at[i], tensor=ypart).wait_recv()
            return y[i, a].astype(F32)

        def add(zs, ys, a, *terms):
            total = p[zs, ys, a].astype(F32)
            for t in terms:
                total = total + t
            p[zs, ys, a] = total.astype(BF)

        def ends(st, k, sign):
            j = 0 if sign > 0 else 1
            to = r0.at[j, st - 1] if k == 0 else r1.at[j, st - 3]
            i = 6 + (st - 1) * 2 + j if k == 0 else 14 + (st - 3) * 2 + j
            return (to.at[cut(sign)] if st == 1 or (st == 3 and k == 1) else to), i

        def send(st, k, sign):
            zs, ys = place(5 - st, k, sign)
            v = p.at[zs, ys]
            if st == 1 or (st == 3 and k == 1):
                v = p.at[zs, ys, cut(sign)]
            to, i = ends(st, k, sign)
            push(v, to, ss.at[i], rs.at[i], tensor=zdev(sign))

        def wait(st, k, sign):
            v, i = ends(st, k, sign)
            copy(v, v, ss.at[i], rs.at[i], tensor=zdev(sign)).wait_recv()
            return v[...].astype(F32)

        def first():
            zs, ys = place(4, 0, 1)
            add(zs, ys, whole, side(4))
            for sign in DIRS:
                send(1, 0, sign)

        def step(st, sign):
            zs, ys = place(4 - st, 0, sign)
            if st == 1:
                add(zs, ys, whole, side(3, sign))
                add(zs, ys, cut(sign), wait(1, 0, sign))
            elif st == 2:
                add(zs, ys, cut(-sign), side(2, sign))
                add(zs, ys, whole, wait(2, 0, sign))
            else:
                add(zs, ys, whole, wait(3, 0, sign))
            send(st + 1, 0, sign)

        def near(sign):
            zs, ys = place(1, 1, sign)
            add(zs, ys, cut(sign), wait(3, 1, sign))
            send(4, 1, sign)

        def total(k):
            zs, ys = spot(z, k)
            return p[zs, ys].astype(F32) + (wait(4, k, 1) + wait(4, k, -1))

        def cross():
            p[z, 1 - yh] = total(1).astype(BF)
            send_side(0)

        def finish():
            return total(0) + side(0)

        task(q + "side4", call(send_side, 4))
        task(q + "first", first)
        task(q + "cross", cross)
        for g in DIRS:
            task(name(q + "side3,", g), call(send_side, 3, g))
            task(name(q + "side2,", g), call(send, 3, 1, g), call(send_side, 2, g))
            task(name(q + "near,", g), call(near, g))
            for st in (1, 2, 3):
                task(name(q + "step", st, g), call(step, st, g))
        return finish

    def group_sum(q, make, p, r, y, ss, rs):
        rows_n = p.shape[1]
        half = rows_n // 2

        def where(xx, k):
            return lax.rem(xx + NX, NX) * 2 + (yl if k == 0 else 1 - yl)

        def number(st, k, sign):
            return (st - 1) * 4 + k * 2 + (0 if sign > 0 else 1)

        def ends(st, k, sign):
            to = r.at[0 if sign > 0 else 1, st - 1, k]
            return to.at[pl.ds(0 if sign > 0 else half, half)] if st == 1 else to

        def send(st, k, sign):
            v = p.at[where(x + sign * (3 - st), k)]
            if st == 1:
                v = v.at[pl.ds(0 if sign > 0 else half, half)]
            i = number(st, k, sign)
            push(v, ends(st, k, sign), ss.at[i], rs.at[i], dp=xdev(sign))

        def wait(st, k, sign):
            v = ends(st, k, sign)
            i = number(st, k, sign)
            copy(v, v, ss.at[i], rs.at[i], dp=xdev(sign)).wait_recv()

        def step(k, sign):
            wait(1, k, sign)
            s = where(x + sign, k)
            a = pl.ds(0 if sign > 0 else half, half)
            j = 0 if sign > 0 else 1
            p[s, a] = (p[s, a].astype(F32) + r[j, 0, k, a].astype(F32)).astype(BF)
            send(2, k, sign)

        def total(k):
            for sign in DIRS:
                wait(2, k, sign)
            return p[where(x, k)].astype(F32) + (r[0, 1, k].astype(F32) + r[1, 1, k].astype(F32))

        def cross():
            p[where(x, 1)] = total(1).astype(BF)
            push(p.at[where(x, 1)], y, ss.at[8], rs.at[8], dp=ylpart)

        def finish():
            own = total(0)
            copy(y, y, ss.at[8], rs.at[8], dp=ylpart).wait_recv()
            return own + y[...].astype(F32)

        def start(k):
            for g in DIRS:
                send(1, k, g)

        for k in (0, 1):
            for dx in (2, 1, -1, 0):
                task(q + "g%d,%d" % (dx, k), call(lambda dx, k: make(where(x + dx, k)), dx, k))
            task(q + "send1,%d" % k, call(start, k))
            for g in DIRS:
                task(name(q + "step,", k, g), call(step, k, g))
        task(q + "cross", cross)
        return finish

    m_finish = scatter("M", pm, rm0, rm1, ym, zm_s, zm_r)
    n_finish = scatter("N", pd, rd0, rd1, yd, zd_s, zd_r)

    waited = set()

    def once(key, src, dst, i):
        if key not in waited:
            waited.add(key)
            copy(src, dst, cp_s.at[i], cp_r.at[i], dp=cpart).wait_recv()

    def out_grads(s):
        once("gout", pgout, pgout, 2)
        once("att", att_far, att_far, 1)
        sgo[s] = (nn(att_own[...], gout[s, core]) + nn(att_far[...], pgout[s])).astype(BF)

    def query_grads(s):
        once("acts", pacts, pacts, 0)
        once("dq", dq_far, dq_far, 3)
        sgw[s] = (nn(dq_own[...], acts[s, core]) + nn(dq_far[...], pacts[s])).astype(BF)

    def key_grads(s):
        once("acts", pacts, pacts, 0)
        once("dk", dk_far, dk_far, 4)
        sgv[s] = (nn(dk_own[...], acts[s, core]) + nn(dk_far[...], pacts[s])).astype(BF)

    o_finish = group_sum("O", out_grads, sgo, xgo, ygo, xo_s, xo_r)
    w_finish = group_sum("W", query_grads, sgw, xgw, ygw, xw_s, xw_r)
    v_finish = group_sum("V", key_grads, sgv, xgv, ygv, xv_s, xv_r)

    outs = []

    def emit(src, to):
        c = pltpu.make_async_copy(src, to, out_sem.at[len(outs)])
        c.start()
        outs.append(c)

    def end_mixed():
        mixed_out[0] = m_finish().astype(BF)
        emit(mixed_out, mixed_hbm)

    def end_out():
        go_out[...] = o_finish()
        emit(go_out, go_hbm)

    def end_query():
        gq_out[...] = w_finish().T
        emit(gq_out, gq_hbm)

    def end_key():
        gkv_out[...] = v_finish()
        emit(gkv_out, gkv_hbm)

    def end_down():
        scaled_rows[...] = n_finish().T * gain_of(me)

    def end_tokens():
        pr_wait()
        inv = lane_inv[:, pl.ds(0, 1)]
        proj = jnp.broadcast_to(jnp.sum(pr[...], axis=0)[:1], (128, TOK)).T[:, :1]
        slope = inv * inv * inv * proj / (FEAT * 16)
        dtok_out[0] = (inv * scaled_rows[...] - tok_ref[0].astype(F32) * slope).astype(BF)
        emit(dtok_out, dtok_hbm)

    task("Mfin", end_mixed)
    task("Ofin", end_out)
    task("Wfin", end_query)
    task("Vfin", end_key)
    task("Nfin", end_down)
    task("out", end_tokens)

    listed = list(tasks.values())
    assert sorted(ORDER) == list(range(len(listed)))
    for number in ORDER:
        for step in listed[number]:
            step()

    for c in sent:
        c.wait_send()
    mg_drain()
    kv_drain()
    dk_drain()
    pr_drain()
    for c in outs:
        c.wait()


def spread(mixed, dtok, gq, gkv, go, mixed_to, dtok_to, gq_to, gk_to, gv_to, go_to):
    mixed_to[...] = mixed[...]
    dtok_to[...] = dtok[...]
    gq_to[...] = gq[...]
    go_to[...] = go[...]
    gk_to[...] = gkv[pl.ds(0, KC), :]
    gv_to[...] = gkv[pl.ds(KC, KC), :]


def body(
    tokens, norm_gain, w_query, w_key, w_value, w_output, positions, scale_exps, loss_exp, out_grad
):
    vmem = pl.BlockSpec(memory_space=pltpu.VMEM)
    smem = pl.BlockSpec(memory_space=pltpu.SMEM)
    hbm = pl.BlockSpec(memory_space=pl.ANY)
    V = pltpu.VMEM
    dma = pltpu.SemaphoreType.DMA
    S = jax.ShapeDtypeStruct
    sums = [
        V((8, 2, TOK, FEAT), BF), V((2, 4, TOK, FEAT), BF), V((2, 2, TOK, FEAT), BF),
        V((6, TOK, FEAT), BF),
    ]
    sums_down = [
        V((8, 2, FEAT, TOK), BF), V((2, 4, FEAT, TOK), BF), V((2, 2, FEAT, TOK), BF),
        V((6, FEAT, TOK), BF),
    ]
    def by_group(n):
        return V((8, n, FEAT), BF), V((2, 2, 2, n, FEAT), BF), V((n, FEAT), BF)

    parts = pl.pallas_call(
        kernel,
        out_shape=(
            S((1, TOK, FEAT), BF), S((1, TOK, FEAT), BF), S((FEAT, QC), F32),
            S((2 * KC, FEAT), F32), S((QC, FEAT), F32),
        ),
        in_specs=[smem, smem, vmem, vmem, vmem, vmem, hbm, hbm, hbm, hbm],
        out_specs=(hbm,) * 5,
        scratch_shapes=[
            V((1, TOK, FEAT), BF), V((1, TOK, FEAT), BF), V((FEAT, QC), F32), V((QC, FEAT), F32),
            V((2 * KC, FEAT), F32),
            V((8192, QC), BF), V((KC, 8192), BF), V((KC, 8192), BF), V((8192, 2 * KC), BF),
            V((QC, 8192), BF),
            V((8, 2, TOK, FEAT), BF), V((8, 2, TOK, FEAT), BF), V((8, 2, TOK, FEAT), BF),
            V((8, TOK, FEAT), BF), V((8, TOK, FEAT), BF),
            *sums, *sums_down,
            *by_group(QC), *by_group(QC), *by_group(64),
            V((QC, TOK), BF), V((QC, TOK), BF), V((QC, TOK), BF), V((QC, TOK), BF),
            V((64, TOK), BF), V((64, TOK), BF),
            V((2, TOK, TOK), F32), V((2, HD, TOK), F32), V((HD, TOK), F32), V((TOK, HD), BF),
            V((TOK, 128), F32), V((2, 64, TOK), F32), V((TOK, TOK), F32), V((TOK, FEAT), F32),
            V((16, 8, 128), F32), V((4, 16, TOK), BF), V((16, 16, TOK), BF),
            V((16, 16, TOK), BF), V((16, 16, TOK), BF), V((16, 8, TOK), F32),
            V((TOK, QC), F32), V((TOK, 2 * KC), F32), V((QC, TOK), F32),
            dma((4,)), dma((5,)),
            dma((22,)), dma((22,)), dma((22,)), dma((22,)),
            dma((18,)), dma((18,)), dma((18,)), dma((18,)),
            dma((9,)), dma((9,)), dma((9,)), dma((9,)), dma((9,)), dma((9,)),
            dma((4, 16)), dma((4, 16)), dma((5,)), dma((5,)),
        ],
        compiler_params=pltpu.CompilerParams(
            collective_id=0, has_side_effects=True, vmem_limit_bytes=60 * 1024 * 1024
        ),
    )(
        scale_exps, loss_exp, tokens, norm_gain, positions, out_grad,
        w_query, w_key.T, w_value.T, w_output,
    )
    mixed, d_rows, grad_query, grad_key, grad_value, grad_output = pl.pallas_call(
        spread,
        out_shape=(
            S((1, TOK, FEAT), BF), S((1, TOK, FEAT), BF), S((FEAT, QC), F32),
            S((KC, FEAT), F32), S((KC, FEAT), F32), S((QC, FEAT), F32),
        ),
        in_specs=[vmem] * 5,
        out_specs=(vmem,) * 6,
    )(*parts)
    return mixed, d_rows, grad_query, grad_key.T, grad_value.T, grad_output


def solution(mesh):
    placed = (
        P("dp", None, "tensor"),
        P("tensor"),
        P(None, "tensor"),
        P(None, "tensor"),
        P(None, "tensor"),
        P("tensor", None),
        P("dp", None),
        P(),
        P(),
        P("dp", None, "tensor"),
    )
    return jax.shard_map(
        body,
        mesh=mesh,
        in_specs=placed,
        out_specs=(
            P("dp", None, "tensor"),
            P("dp", None, "tensor"),
            P("dp", "tensor"),
            P("dp", "tensor"),
            P("dp", "tensor"),
            P("tensor", "dp"),
        ),
        check_vma=False,
    )
```

```python
import functools
import math

import jax
import jax.numpy as jnp
from jax import lax
from jax.experimental import pallas as pl
from jax.experimental.pallas import tpu as pltpu
from jax.sharding import PartitionSpec as P

HD = 128
E4_TOP = 448.0
E5_TOP = 57344.0
BF = jnp.bfloat16
F32 = jnp.float32
MESH = pl.DeviceIdType.MESH
NZ, NX, TOK, FEAT, QC, KC = 8, 4, 128, 512, 256, 32
DIRS = (1, -1)


def nn(a, b):
    return jnp.dot(a, b, preferred_element_type=F32)


def nt(a, b):
    return lax.dot_general(a, b, (((1,), (1,)), ((), ())), preferred_element_type=F32)


def halves(a):
    high = a.astype(BF)
    return high, (a - high.astype(F32)).astype(BF)


def precise(dot, a, b):
    ah, al = halves(a)
    bh, bl = halves(b)
    return dot(ah, bh) + (dot(ah, bl) + dot(al, bh))


def power_of_half(e):
    out = jnp.float32(1.0)
    for bit in range(5):
        out = out * jnp.where(((e >> bit) & 1) == 1, jnp.float32(2.0 ** -(1 << bit)), jnp.float32(1.0))
    return out


def clip(v, limit):
    return jnp.minimum(jnp.maximum(v, -limit), limit)


def rot(v, c, s):
    return jnp.concatenate([v[:64] * c - v[64:] * s, v[64:] * c + v[:64] * s], axis=0)


def unrot(v, c, s):
    return jnp.concatenate([v[:64] * c + v[64:] * s, v[64:] * c - v[:64] * s], axis=0)


ORDER = (
    0, 46, 3, 13, 1, 5, 15, 2, 4, 14, 19, 47, 8, 116, 76, 126, 131, 96, 106, 56, 101, 111, 6, 16,
    23, 61, 66, 86, 121, 71, 91, 81, 57, 18, 9, 60, 75, 100, 7, 10, 21, 70, 105, 55, 65, 17, 20,
    85, 11, 80, 36, 24, 95, 26, 25, 38, 97, 67, 28, 62, 110, 115, 12, 22, 90, 31, 37, 42, 27, 125,
    102, 120, 41, 107, 29, 72, 32, 39, 77, 130, 44, 48, 30, 33, 49, 117, 34, 82, 40, 112, 87, 43,
    35, 45, 92, 122, 50, 127, 108, 133, 138, 123, 113, 140, 98, 103, 73, 78, 88, 63, 118, 151, 83,
    68, 58, 93, 128, 132, 52, 53, 51, 152, 142, 139, 141, 150, 143, 154, 153, 136, 193, 186, 194,
    195, 188, 187, 196, 189, 54, 134, 163, 124, 129, 94, 114, 119, 175, 164, 176, 165, 89, 84, 109,
    104, 177, 79, 74, 197, 166, 99, 69, 64, 59, 147, 158, 135, 168, 203, 178, 167, 190, 137, 179,
    155, 144, 201, 204, 198, 199, 148, 180, 159, 202, 169, 162, 208, 161, 183, 172, 192, 191, 145,
    156, 149, 181, 170, 160, 207, 173, 184, 200, 146, 157, 182, 171, 174, 185, 205, 206, 209, 210,
)


def kernel(
    scale_ref, loss_ref, tok_hbm, gain_hbm, pos_hbm, og_hbm, wq_hbm, wk_hbm, wv_hbm, wo_hbm,
    mixed_hbm, dtok_hbm, gq_hbm, gkv_hbm, go_hbm,
    mixed_out, dtok_out, gq_out, go_out, gkv_out,
    wq, wkt, wvt, wkv, wo, toks, acts, gout, pgout,
    pm, rm, pd, rd,
    sgo, xgo, ygo, actr, dqr, dkr_all, w_send, w_own, w_far, v_send, v_own, v_far,
    att_own, att_far, dq_own, dk_own, probs, q_rot, k_rot, v_rows, lane_inv,
    angles, projected, scaled_rows, gain_ref, pos_ref,
    mg, kvs, kvr, dks, dkr, pr,
    qacc, kvacc, dacc,
    load_sem, out_sem, gt_s, gt_r, gg_s, gg_r, zm_s, zm_r, zd_s, zd_r, xo_s, xo_r,
    aa_s, aa_r, dq_s, dq_r, dk_s, dk_r, sm_s, sm_r, cp_s, cp_r,
):
    dp = lax.axis_index("dp")
    me = lax.axis_index("tensor")
    z, yh = me // 2, lax.rem(me, 2)
    x, yl, core = dp // 4, lax.rem(dp // 2, 2), lax.rem(dp, 2)
    sent = []
    tasks = {}
    K_ORDER = (1, 0)
    SLOTS = [(d, k, g) for k in (0, 1) for d in range(5) for g in (DIRS if 0 < d < 4 else (1,))]

    def name(head, *parts):
        return head + ",".join(("+" if v > 0 else "-") if n == len(parts) - 1 else str(v) for n, v in enumerate(parts))

    def task(key, *steps):
        tasks[key] = steps

    def call(f, *args):
        return functools.partial(f, *args)

    def copy(src, dst, ssem, rsem, **where):
        return pltpu.make_async_remote_copy(
            src_ref=src, dst_ref=dst, send_sem=ssem, recv_sem=rsem,
            device_id=where, device_id_type=MESH,
        )

    def push(*args, **where):
        c = copy(*args, **where)
        c.start()
        sent.append(c)

    def zdev(sign):
        return lax.rem(z + sign + NZ, NZ) * 2 + yh

    def xdev(sign):
        return lax.rem(x + sign + NX, NX) * 4 + yl * 2 + core

    ypart = z * 2 + (1 - yh)
    ylpart = x * 4 + (1 - yl) * 2 + core
    cpart = x * 4 + yl * 2 + (1 - core)

    def near(n, sign):
        return lax.rem(x + sign * (n // 2) + NX, NX), (core if n % 2 == 0 else 1 - core)

    def near_dp(n, sign):
        xs, cs = near(n, sign)
        return xs * 4 + yl * 2 + cs

    first_load = pltpu.make_async_copy(tok_hbm.at[0], toks.at[z, yh], load_sem.at[4])
    first_load.start()
    loads = [
        pltpu.make_async_copy(wk_hbm, wkt, load_sem.at[0]),
        pltpu.make_async_copy(wv_hbm, wvt, load_sem.at[1]),
        pltpu.make_async_copy(wq_hbm, wq, load_sem.at[2]),
        pltpu.make_async_copy(wo_hbm, wo, load_sem.at[3]),
    ]
    grad_load = pltpu.make_async_copy(og_hbm.at[0], gout.at[z, yh], load_sem.at[5])
    gain_load = pltpu.make_async_copy(gain_hbm, gain_ref, load_sem.at[6])
    pos_load = pltpu.make_async_copy(pos_hbm, pos_ref, load_sem.at[7])
    grad_load.start()
    gain_load.start()
    pos_load.start()
    for c in loads:
        c.start()

    barrier = pltpu.get_barrier_semaphore()

    def greet(o, carry):
        pl.semaphore_signal(
            barrier, inc=1, device_id={"tensor": lax.rem(me + o, 16)}, device_id_type=MESH
        )
        return carry

    lax.fori_loop(1, 16, greet, 0)
    for other in [near_dp(n, 1) for n in range(1, 8)] + [ylpart]:
        pl.semaphore_signal(barrier, inc=1, device_id={"dp": other}, device_id_type=MESH)

    lims = [E4_TOP * power_of_half(scale_ref[i]) for i in range(6)]
    glim = E5_TOP * power_of_half(scale_ref[6] + loss_ref[0])

    def as_row(column):
        return jnp.broadcast_to(column, (TOK, 128)).T

    first_load.wait()
    pl.semaphore_wait(barrier, 23)

    def spot(zz, k):
        return lax.rem(zz + NZ, NZ), (yh if k == 0 else 1 - yh)

    def half_of(sign):
        return pl.ds(0 if sign > 0 else TOK // 2, TOK // 2)

    def gather(p, buf, ss, rs, prepare=None):
        def part(zz, k, h):
            zs, ys = spot(zz, k)
            return buf.at[zs, ys, pl.ds(h * 64, 64)]

        def carried(g):
            return 0 if g > 0 else 1

        first = {(1, 0): 0, (2, 0): 4, (3, 0): 8, (4, 0): 12, (1, 1): 14, (2, 1): 18}

        def ring(d, k, g, h):
            i = first[d, k] + (0 if g > 0 else 1)
            return i if (d, k) in ((4, 0), (2, 1)) else i + 2 * h

        def send(d, k, g, h):
            v, i = part(z - g * (d - 1), k, h), ring(d, k, g, h)
            push(v, v, ss.at[i], rs.at[i], tensor=zdev(g))

        def wait(d, k, g, h):
            v, i = part(z - g * d, k, h), ring(d, k, g, h)
            copy(v, v, ss.at[i], rs.at[i], tensor=zdev(g)).wait_recv()

        def side(d, g, h):
            if d == 0:
                return 20 + h
            return {2: 22, 3: 24, 4: 28}[d] + (0 if g > 0 else 1) + (2 * h if d == 3 else 0)

        def send_side(d, g, h):
            v, i = part(z - g * d, 0, h), side(d, g, h)
            push(v, v, ss.at[i], rs.at[i], tensor=ypart)

        def wait_side(d, g, h):
            v, i = part(z - g * d, 1, h), side(d, g, h)
            copy(v, v, ss.at[i], rs.at[i], tensor=ypart).wait_recv()

        def begin():
            if prepare is not None:
                prepare()
            for h in (0, 1):
                send_side(0, 1, h)
                for g in DIRS:
                    send(1, 0, g, h)

        def partner(h):
            wait_side(0, 1, h)
            for g in DIRS:
                send(1, 1, g, h)

        task(p + "0", begin)
        for h in (0, 1):
            task(p + "f11%d" % h, call(partner, h))
        for g in DIRS:
            n = "+" if g > 0 else "-"
            c = carried(g)
            for h in (0, 1):
                task(p + "f20%s%d" % (n, h), call(wait, 1, 0, g, h), call(send, 2, 0, g, h))
                task(p + "f30%s%d" % (n, h), call(wait, 2, 0, g, h), call(send, 3, 0, g, h))
            task(p + "f40" + n, call(wait, 3, 0, g, c), call(send, 4, 0, g, c))
            task(p + "f21" + n, call(wait, 1, 1, g, c), call(send, 2, 1, g, c))
            task(p + "s2" + n, call(send_side, 2, g, 1 - c))
            task(p + "s3%s%d" % (n, c), call(send_side, 3, g, c))
            task(p + "s3%s%d" % (n, 1 - c), call(wait, 3, 0, g, 1 - c), call(send_side, 3, g, 1 - c))
            task(p + "s4" + n, call(wait, 4, 0, g, c), call(send_side, 4, g, c))

        def arrived(d, k, g):
            c = carried(g)
            if (d, k) == (1, 1):
                wait(1, 1, g, 1 - c)
            elif (d, k) == (2, 1):
                wait(2, 1, g, c)
                wait_side(2, g, 1 - c)
            elif (d, k) == (3, 1):
                wait_side(3, g, 0)
                wait_side(3, g, 1)
            elif (d, k) == (4, 1):
                for other in DIRS:
                    wait_side(4, other, carried(other))

        return arrived

    def exchange(src, dst, j):
        def start(o, carry):
            peer = lax.rem(me + o, 16)
            copy(src(peer), dst.at[me], sm_s.at[j, o], sm_r.at[j, o], tensor=peer).start()
            return carry

        def recv(o, carry):
            origin = lax.rem(me + 16 - o, 16)
            copy(src(me), dst.at[origin], sm_s.at[j, o], sm_r.at[j, o], tensor=origin).wait_recv()
            return carry

        def drain(o, carry):
            peer = lax.rem(me + o, 16)
            copy(src(peer), dst.at[me], sm_s.at[j, o], sm_r.at[j, o], tensor=peer).wait_send()
            return carry

        return (
            lambda: lax.fori_loop(1, 16, start, 0),
            lambda: lax.fori_loop(1, 16, recv, 0),
            lambda: lax.fori_loop(1, 16, drain, 0),
        )

    mg_start, mg_wait, mg_drain = exchange(lambda peer: mg.at[me], mg, 0)
    kv_start, kv_wait, kv_drain = exchange(lambda peer: kvs.at[peer // 4], kvr, 1)
    dk_start, dk_wait, dk_drain = exchange(lambda peer: dks.at[peer], dkr, 2)
    pr_start, pr_wait, pr_drain = exchange(lambda peer: pr.at[me], pr, 3)

    t_arrived = gather("T", toks, gt_s, gt_r)

    def cast_grad():
        grad_load.wait()
        gout[z, yh] = clip(gout[z, yh].astype(F32), glim).astype(BF)

    g_arrived = gather("G", gout, gg_s, gg_r, cast_grad)

    def send_squares():
        gain_load.wait()
        gain = gain_ref[...].astype(F32).reshape(1, FEAT)
        lanes = [gain[:, i * 128 : (i + 1) * 128] for i in range(4)]
        rows = toks[z, yh].astype(F32)
        squares = as_row(jnp.sum(rows * rows, axis=1, keepdims=True))[:4]
        mg[me] = jnp.concatenate(lanes + [squares], axis=0)
        mg_start()

    task("mg", send_squares)

    def gain_of(slot):
        g = mg[slot]
        return jnp.concatenate([g[i : i + 1] for i in range(4)], axis=1)

    def prepare():
        pos_load.wait()
        pair = lax.broadcasted_iota(jnp.int32, (64, TOK), 0).astype(F32)
        angle = pos_ref[...].astype(F32) * jnp.exp(pair * (-2.0 * math.log(500000.0) / HD))
        angles[0] = jnp.cos(angle)
        angles[1] = jnp.sin(angle)
        for total in (qacc, kvacc, dacc, projected):
            total[...] = jnp.zeros_like(total)
        mg_wait()
        squares = jnp.sum(mg[...], axis=0)[4:5]
        inv_row = lax.rsqrt(squares / (FEAT * 16) + 1e-05)
        lane_inv[...] = jnp.broadcast_to(inv_row[:1], (128, TOK)).T
        for c in loads:
            c.wait()

    task("pre", prepare)

    def block(d, k, g):
        zs, ys = spot(z - g * d, k)
        return zs, ys, pl.ds(pl.multiple_of((zs * 2 + ys) * 512, 512), 512)

    def act_copy(zs, ys):
        return copy(
            acts.at[zs, ys], actr.at[x * 2 + core, lax.rem(zs, 2)],
            aa_s.at[zs * 2 + ys], aa_r.at[(x * 2 + core) * 2 + lax.rem(zs, 2)],
            dp=(zs // 2) * 4 + yl * 2 + ys,
        )

    def project(d, k, g):
        t_arrived(d, k, g)
        zs, ys, r = block(d, k, g)
        inv = lane_inv[:, pl.ds(0, 1)]
        a = toks[zs, ys].astype(F32) * inv * gain_of(zs * 2 + ys)
        a = clip(a, lims[0]).astype(BF)
        acts[zs, ys] = a

        @pl.when(jnp.logical_or(zs // 2 != x, ys != core))
        def _():
            act_copy(zs, ys).start()

        w = clip(wq[r, :].astype(F32), lims[1]).astype(BF)
        wq[r, :] = w
        wn = jnp.concatenate(
            [clip(wkt[:, r].astype(F32), lims[2]), clip(wvt[:, r].astype(F32), lims[3])], axis=0
        ).T.astype(BF)
        wkv[r, :] = wn
        qacc[...] += nn(a, w)
        kvacc[...] += nn(a, wn)

    def cast_out(d, k, g):
        zs, ys, r = block(d, k, g)
        wo[:, r] = clip(wo[:, r].astype(F32), lims[4]).astype(BF)

    def back(d, k, g):
        g_arrived(d, k, g)
        zs, ys, r = block(d, k, g)
        dacc[...] += nt(wo[:, r], gout[zs, ys])

    def natural(i):
        low = i & 31
        return (low & 3) * 16 + (i >> 5) * 8 + (low >> 2)

    i0 = lax.broadcasted_iota(jnp.int32, (64, 64), 0)
    i1 = lax.broadcasted_iota(jnp.int32, (64, 64), 1)

    def send_kv():
        by_head = jnp.where(natural(i1) == i0, 1.0, 0.0).astype(BF)
        kvs[...] = nt(by_head, kvacc[...].astype(BF)).astype(BF).reshape(4, 16, TOK)
        kv_start()
        kvr[me] = kvs[me // 4]

    task("kv", send_kv)

    def turn_query():
        q_t = qacc[...].astype(BF).astype(F32).T
        for h in range(2):
            q_rot[h] = rot(q_t[h * HD : (h + 1) * HD], angles[0], angles[1])

    task("qrot", turn_query)

    def attend():
        kv_wait()
        kv = kvr[...].astype(F32)
        k_t = kv[:, :8].reshape(HD, TOK)
        v_t = kv[:, 8:].reshape(HD, TOK)
        k_turned = rot(k_t, angles[0], angles[1])
        k_rot[...] = k_turned
        k_rows = k_turned.T
        v_t16 = v_t.astype(BF)
        v_rows[...] = v_t.T.astype(BF)
        src = lax.broadcasted_iota(jnp.int32, (TOK, TOK), 0)
        dst = lax.broadcasted_iota(jnp.int32, (TOK, TOK), 1)
        allowed = (src <= dst) & (src >= dst - pos_ref[...])
        for h in range(2):
            score = precise(nn, k_rows, q_rot[h]) * (1.0 / math.sqrt(HD))
            weight = jnp.where(allowed, jnp.exp(jnp.where(allowed, score, 0.0)), 0.0)
            p = weight / jnp.sum(weight, axis=0, keepdims=True)
            probs[h] = p
            att = nn(v_t16, p.astype(BF)).astype(BF).astype(F32)
            att_own[pl.ds(h * HD, HD), :] = clip(att, lims[5]).astype(BF)
        push(att_own, att_far, cp_s.at[1], cp_r.at[1], dp=cpart)

    task("att", attend)

    def mix(d, k, g):
        zs, ys, r = block(d, k, -g)
        att_rows = att_own[...].astype(F32).T.astype(BF)
        pm[zs, ys] = nn(att_rows, wo[:, r]).astype(BF)

    def share_gout():
        push(gout.at[:, 1 - core], pgout, cp_s.at[2], cp_r.at[2], dp=cpart)

    task("gpush", share_gout)

    def score_grad(h):
        g = dacc[pl.ds(h * HD, HD), :].astype(BF)
        dw = nn(v_rows[...], g)
        p = probs[h]
        delta = jnp.sum(p * dw, axis=0, keepdims=True)
        return g, p, p * (dw - delta) * (1.0 / math.sqrt(HD))

    def backward():
        dk_rot = jnp.zeros((HD, TOK), F32)
        dv_t = jnp.zeros((HD, TOK), F32)
        for h in range(2):
            g, p, ds = score_grad(h)
            p_high, p_low = halves(p)
            dv_t = dv_t + nt(g, p_high) + nt(g, p_low)
            dk_rot = dk_rot + precise(nt, q_rot[h], ds)
            probs[h] = ds
        dk_t = unrot(dk_rot, angles[0], angles[1])
        dks[...] = jnp.concatenate(
            [dk_t.reshape(16, 8, TOK), dv_t.reshape(16, 8, TOK)], axis=1
        ).astype(BF)
        dk_start()
        dkr[me] = dks[me]

    task("bwd", backward)

    def to_row(src, to, ss, rs):
        for n in range(1, 8):
            push(src, to.at[x * 2 + core], ss.at[n], rs.at[n], dp=near_dp(n, 1))

    def query_grad():
        for h in range(2):
            dq = unrot(precise(nn, k_rot[...], probs[h]), angles[0], angles[1])
            dq_own[pl.ds(h * HD, HD), :] = dq.astype(BF)
        to_row(dq_own, dqr, dq_s, dq_r)

    task("bwq", query_grad)

    def key_grad():
        dk_wait()
        by_column = jnp.where(natural(i0) == i1, 1.0, 0.0).astype(BF)
        dkv = jnp.sum(dkr[...].astype(F32).reshape(4, 4, 16, TOK), axis=1).reshape(64, TOK)
        dk_own[...] = nn(by_column, dkv.astype(BF)).astype(BF)
        to_row(dk_own, dkr_all, dk_s, dk_r)

    task("dkfin", key_grad)

    def down(d, k, g):
        zs, ys, r = block(d, k, -g)
        term = (nn(wq[r, :], dq_own[...]) + nn(wkv[r, :], dk_own[...])).astype(BF)
        pd[zs, ys] = term
        high, low = halves(toks[zs, ys].astype(F32) * gain_of(zs * 2 + ys))
        projected[...] += nn(high, term) + nn(low, term)

    for d, k, g in SLOTS:
        task(name("proj", d, k, g), call(project, d, k, g))
        task(name("clipo", d, k, g), call(cast_out, d, k, g))
        task(name("back", d, k, g), call(back, d, k, g))
        task(name("mix", d, k, g), call(mix, d, k, g))
        task(name("down", d, k, g), call(down, d, k, g))

    def send_product():
        diagonal = lax.broadcasted_iota(jnp.int32, (TOK, TOK), 0) == lax.broadcasted_iota(
            jnp.int32, (TOK, TOK), 1
        )
        own = jnp.sum(jnp.where(diagonal, projected[...], 0.0), axis=0, keepdims=True)
        pr[me] = jnp.broadcast_to(own, (8, TOK))
        pr_start()

    task("prx", send_product)

    def scatter(q, p, r, ss, rs):
        half = p.shape[2] // 2
        first = {(3, 1): 0, (4, 1): 2, (1, 0): 6, (2, 0): 8, (3, 0): 12, (4, 0): 16}

        def area(h):
            return pl.ds(h * half, half)

        def place(d, k, g):
            return spot(z + g * d, k)

        def ring(st, k, g, h):
            i = first[st, k] + (0 if g > 0 else 1)
            return i if (st, k) in ((3, 1), (1, 0)) else i + 2 * h

        def side(d, g, h):
            if d in (0, 4):
                return (28 if d == 0 else 20) + h
            return {3: 22, 2: 26}[d] + (0 if g > 0 else 1) + (2 * h if d == 3 else 0)

        def send(st, k, g, h):
            zs, ys = place(5 - st, k, g)
            i = ring(st, k, g, h)
            push(p.at[zs, ys, area(h)], r.at[i], ss.at[i], rs.at[i], tensor=zdev(g))

        def send_side(d, g, h):
            zs, ys = place(d, 1, g)
            i = side(d, g, h)
            push(p.at[zs, ys, area(h)], r.at[i], ss.at[i], rs.at[i], tensor=ypart)

        def got(st, k, g, h):
            i = ring(st, k, g, h)
            copy(r.at[i], r.at[i], ss.at[i], rs.at[i], tensor=zdev(g)).wait_recv()
            return r[i].astype(F32)

        def got_side(d, g, h):
            i = side(d, g, h)
            copy(r.at[i], r.at[i], ss.at[i], rs.at[i], tensor=ypart).wait_recv()
            return r[i].astype(F32)

        def add(d, k, g, h, *terms):
            zs, ys = place(d, k, g)
            total = p[zs, ys, area(h)].astype(F32)
            for t in terms:
                total = total + t()
            p[zs, ys, area(h)] = total.astype(BF)

        def pieces(k, h):
            return [call(got, 4, k, g, h) for g in DIRS]

        for h in (0, 1):
            task(q + "cross%d" % h, call(add, 0, 1, 1, h, *pieces(1, h)), call(send_side, 0, 1, h))
        task(q + "side4", call(send_side, 4, 1, 0), call(send_side, 4, 1, 1))
        for g in DIRS:
            n = "+" if g > 0 else "-"
            c = 0 if g > 0 else 1
            o = 1 - c
            task(q + "side3" + n, call(send_side, 3, g, c), call(send_side, 3, g, o))
            task(q + "side2" + n, call(send, 3, 1, g, c), call(send_side, 2, g, o))
            task(q + "near%s%d" % (n, o), call(send, 4, 1, g, o))
            task(
                q + "near%s%d" % (n, c),
                call(add, 1, 1, g, c, call(got, 3, 1, g, c)), call(send, 4, 1, g, c),
            )
            task(
                q + "first" + n,
                call(add, 4, 0, g, c, call(got_side, 4, 1, c)), call(send, 1, 0, g, c),
            )
            for h in (0, 1):
                terms = [call(got_side, 3, g, h)] + ([call(got, 1, 0, g, h)] if h == c else [])
                task(
                    q + "step1%s%d" % (n, h), call(add, 3, 0, g, h, *terms), call(send, 2, 0, g, h)
                )
                terms = [call(got, 2, 0, g, h)] + ([call(got_side, 2, g, h)] if h == o else [])
                task(
                    q + "step2%s%d" % (n, h), call(add, 2, 0, g, h, *terms), call(send, 3, 0, g, h)
                )
                task(
                    q + "step3%s%d" % (n, h),
                    call(add, 1, 0, g, h, call(got, 3, 0, g, h)), call(send, 4, 0, g, h),
                )

        def finish():
            total = []
            for h in (0, 1):
                t = p[z, yh, area(h)].astype(F32)
                for piece in pieces(0, h) + [call(got_side, 0, 1, h)]:
                    t = t + piece()
                total.append(t)
            return jnp.concatenate(total, axis=0)

        return finish

    def group_sum(q, make, p, r, y, ss, rs):
        rows_n = p.shape[1]
        half = rows_n // 2

        def where(xx, k):
            return lax.rem(xx + NX, NX) * 2 + (yl if k == 0 else 1 - yl)

        def number(st, k, sign):
            return (st - 1) * 4 + k * 2 + (0 if sign > 0 else 1)

        def ends(st, k, sign):
            to = r.at[0 if sign > 0 else 1, st - 1, k]
            return to.at[pl.ds(0 if sign > 0 else half, half)] if st == 1 else to

        def send(st, k, sign):
            v = p.at[where(x + sign * (3 - st), k)]
            if st == 1:
                v = v.at[pl.ds(0 if sign > 0 else half, half)]
            i = number(st, k, sign)
            push(v, ends(st, k, sign), ss.at[i], rs.at[i], dp=xdev(sign))

        def wait(st, k, sign):
            v = ends(st, k, sign)
            i = number(st, k, sign)
            copy(v, v, ss.at[i], rs.at[i], dp=xdev(sign)).wait_recv()

        def step(k, sign):
            wait(1, k, sign)
            s = where(x + sign, k)
            a = pl.ds(0 if sign > 0 else half, half)
            j = 0 if sign > 0 else 1
            p[s, a] = (p[s, a].astype(F32) + r[j, 0, k, a].astype(F32)).astype(BF)
            send(2, k, sign)

        def total(k):
            for sign in DIRS:
                wait(2, k, sign)
            return p[where(x, k)].astype(F32) + (r[0, 1, k].astype(F32) + r[1, 1, k].astype(F32))

        def cross():
            p[where(x, 1)] = total(1).astype(BF)
            push(p.at[where(x, 1)], y, ss.at[8], rs.at[8], dp=ylpart)

        def finish():
            own = total(0)
            copy(y, y, ss.at[8], rs.at[8], dp=ylpart).wait_recv()
            return own + y[...].astype(F32)

        def start(k):
            for g in DIRS:
                send(1, k, g)

        for k in (0, 1):
            for dx in (2, 1, -1, 0):
                task(q + "g%d,%d" % (dx, k), call(lambda dx, k: make(where(x + dx, k)), dx, k))
            task(q + "send1,%d" % k, call(start, k))
            for g in DIRS:
                task(name(q + "step,", k, g), call(step, k, g))
        task(q + "cross", cross)
        return finish

    m_finish = scatter("M", pm, rm, zm_s, zm_r)
    n_finish = scatter("N", pd, rd, zd_s, zd_r)

    waited = set()

    def once(key, src, dst, i):
        if key not in waited:
            waited.add(key)
            copy(src, dst, cp_s.at[i], cp_r.at[i], dp=cpart).wait_recv()

    def out_grads(s):
        once("gout", pgout, pgout, 2)
        once("att", att_far, att_far, 1)
        sgo[s] = (nn(att_own[...], gout[s, core]) + nn(att_far[...], pgout[s])).astype(BF)

    def act_wait():
        if "acts" not in waited:
            waited.add("acts")
            for n in range(1, 8):
                xs, cs = near(n, -1)
                for side in (0, 1):
                    v = actr.at[xs * 2 + cs, side]
                    i = (xs * 2 + cs) * 2 + side
                    copy(v, v, aa_s.at[n], aa_r.at[i], dp=near_dp(n, -1)).wait_recv()

    def row_sum(q, own, to, ss, rs, out, keep, far, i):
        def product(side):
            act_wait()
            total = nn(own[...], acts[x * 2 + side, core])
            for n in range(1, 8):
                xs, cs = near(n, -1)
                v = to.at[xs * 2 + cs]
                if (q, n) not in waited:
                    waited.add((q, n))
                    copy(v, v, ss.at[n], rs.at[n], dp=near_dp(n, -1)).wait_recv()
                total = total + nn(to[xs * 2 + cs], actr[xs * 2 + cs, side])
            return total

        def give():
            out[...] = product(1 - yl).astype(BF)
            push(out, far, cp_s.at[i], cp_r.at[i], dp=ylpart)

        def hold():
            keep[...] = product(yl)

        def finish():
            copy(far, far, cp_s.at[i], cp_r.at[i], dp=ylpart).wait_recv()
            return keep[...] + far[...].astype(F32)

        task(q + "1", give)
        task(q + "0", hold)
        return finish

    o_finish = group_sum("O", out_grads, sgo, xgo, ygo, xo_s, xo_r)
    w_finish = row_sum("W", dq_own, dqr, dq_s, dq_r, w_send, w_own, w_far, 3)
    v_finish = row_sum("V", dk_own, dkr_all, dk_s, dk_r, v_send, v_own, v_far, 4)

    outs = []

    def emit(src, to):
        c = pltpu.make_async_copy(src, to, out_sem.at[len(outs)])
        c.start()
        outs.append(c)

    def end_mixed():
        mixed_out[0] = m_finish().astype(BF)
        emit(mixed_out, mixed_hbm)

    def end_out():
        go_out[...] = o_finish()
        emit(go_out, go_hbm)

    def end_query():
        gq_out[...] = w_finish().T
        emit(gq_out, gq_hbm)

    def end_key():
        gkv_out[...] = v_finish()
        emit(gkv_out, gkv_hbm)

    def end_down():
        scaled_rows[...] = n_finish().T * gain_of(me)

    def end_tokens():
        pr_wait()
        inv = lane_inv[:, pl.ds(0, 1)]
        proj = jnp.broadcast_to(jnp.sum(pr[...], axis=0)[:1], (128, TOK)).T[:, :1]
        slope = inv * inv * inv * proj / (FEAT * 16)
        dtok_out[0] = (inv * scaled_rows[...] - toks[z, yh].astype(F32) * slope).astype(BF)
        emit(dtok_out, dtok_hbm)

    task("Mfin", end_mixed)
    task("Ofin", end_out)
    task("Wfin", end_query)
    task("Vfin", end_key)
    task("Nfin", end_down)
    task("out", end_tokens)

    def act_drain(slot, carry):
        @pl.when(jnp.logical_or(slot // 4 != x, lax.rem(slot, 2) != core))
        def _():
            act_copy(slot // 2, lax.rem(slot, 2)).wait_send()

        return carry

    listed = list(tasks.values())
    assert sorted(ORDER) == list(range(len(listed)))
    names = list(tasks)
    idle = {"att", "dkfin", "Nfin"} | {key for key in names if key.startswith(("Nstep", "Ncross"))}
    begun = []
    for number in ORDER:
        if names[number] in idle:
            while begun and len(sent) - begun[0] > 24:
                sent_first = begun.pop(0)
                sent[sent_first].wait_send()
        if names[number] == "att":
            mg_drain()
        if names[number] == "dkfin":
            kv_drain()
            lax.fori_loop(0, 16, act_drain, 0)
        if names[number] == "Nfin":
            dk_drain()
        before = len(sent)
        for step in listed[number]:
            step()
        begun.extend(range(before, len(sent)))

    for i in begun:
        sent[i].wait_send()
    pr_drain()
    for c in outs:
        c.wait()


def spread(mixed, dtok, gq, gkv, go, mixed_to, dtok_to, gq_to, gk_to, gv_to, go_to):
    mixed_to[...] = mixed[...]
    dtok_to[...] = dtok[...]
    gq_to[...] = gq[...]
    go_to[...] = go[...]
    gk_to[...] = gkv[pl.ds(0, KC), :]
    gv_to[...] = gkv[pl.ds(KC, KC), :]


def body(
    tokens, norm_gain, w_query, w_key, w_value, w_output, positions, scale_exps, loss_exp, out_grad
):
    vmem = pl.BlockSpec(memory_space=pltpu.VMEM)
    smem = pl.BlockSpec(memory_space=pltpu.SMEM)
    hbm = pl.BlockSpec(memory_space=pl.ANY)
    V = pltpu.VMEM
    dma = pltpu.SemaphoreType.DMA
    S = jax.ShapeDtypeStruct
    sums = [V((8, 2, TOK, FEAT), BF), V((30, TOK // 2, FEAT), BF)]
    sums_down = [V((8, 2, FEAT, TOK), BF), V((30, FEAT // 2, TOK), BF)]

    def by_group(n):
        return V((8, n, FEAT), BF), V((2, 2, 2, n, FEAT), BF), V((n, FEAT), BF)

    parts = pl.pallas_call(
        kernel,
        out_shape=(
            S((1, TOK, FEAT), BF), S((1, TOK, FEAT), BF), S((FEAT, QC), F32),
            S((2 * KC, FEAT), F32), S((QC, FEAT), F32),
        ),
        in_specs=[smem, smem] + [hbm] * 8,
        out_specs=(hbm,) * 5,
        scratch_shapes=[
            V((1, TOK, FEAT), BF), V((1, TOK, FEAT), BF), V((FEAT, QC), F32), V((QC, FEAT), F32),
            V((2 * KC, FEAT), F32),
            V((8192, QC), BF), V((KC, 8192), BF), V((KC, 8192), BF), V((8192, 2 * KC), BF),
            V((QC, 8192), BF),
            V((8, 2, TOK, FEAT), BF), V((8, 2, TOK, FEAT), BF), V((8, 2, TOK, FEAT), BF),
            V((8, TOK, FEAT), BF),
            *sums, *sums_down,
            *by_group(QC),
            V((8, 2, TOK, FEAT), BF), V((8, QC, TOK), BF), V((8, 64, TOK), BF),
            V((QC, FEAT), BF), V((QC, FEAT), F32), V((QC, FEAT), BF),
            V((64, FEAT), BF), V((64, FEAT), F32), V((64, FEAT), BF),
            V((QC, TOK), BF), V((QC, TOK), BF), V((QC, TOK), BF), V((64, TOK), BF),
            V((2, TOK, TOK), F32), V((2, HD, TOK), F32), V((HD, TOK), F32), V((TOK, HD), BF),
            V((TOK, 128), F32), V((2, 64, TOK), F32), V((TOK, TOK), F32), V((TOK, FEAT), F32),
            V((FEAT,), BF), V((1, TOK), jnp.int32),
            V((16, 8, 128), F32), V((4, 16, TOK), BF), V((16, 16, TOK), BF),
            V((16, 16, TOK), BF), V((16, 16, TOK), BF), V((16, 8, TOK), F32),
            V((TOK, QC), F32), V((TOK, 2 * KC), F32), V((QC, TOK), F32),
            dma((8,)), dma((5,)),
            dma((30,)), dma((30,)), dma((30,)), dma((30,)),
            dma((30,)), dma((30,)), dma((30,)), dma((30,)),
            dma((9,)), dma((9,)), dma((16,)), dma((16,)), dma((8,)), dma((8,)), dma((8,)), dma((8,)),
            dma((4, 16)), dma((4, 16)), dma((5,)), dma((5,)),
        ],
        compiler_params=pltpu.CompilerParams(
            collective_id=0, has_side_effects=True, vmem_limit_bytes=60 * 1024 * 1024
        ),
    )(
        scale_exps, loss_exp, tokens, norm_gain, positions, out_grad,
        w_query, w_key.T, w_value.T, w_output,
    )
    mixed, d_rows, grad_query, grad_key, grad_value, grad_output = pl.pallas_call(
        spread,
        out_shape=(
            S((1, TOK, FEAT), BF), S((1, TOK, FEAT), BF), S((FEAT, QC), F32),
            S((KC, FEAT), F32), S((KC, FEAT), F32), S((QC, FEAT), F32),
        ),
        in_specs=[vmem] * 5,
        out_specs=(vmem,) * 6,
    )(*parts)
    return mixed, d_rows, grad_query, grad_key.T, grad_value.T, grad_output


def solution(mesh):
    placed = (
        P("dp", None, "tensor"),
        P("tensor"),
        P(None, "tensor"),
        P(None, "tensor"),
        P(None, "tensor"),
        P("tensor", None),
        P("dp", None),
        P(),
        P(),
        P("dp", None, "tensor"),
    )
    return jax.shard_map(
        body,
        mesh=mesh,
        in_specs=placed,
        out_specs=(
            P("dp", None, "tensor"),
            P("dp", None, "tensor"),
            P("dp", "tensor"),
            P("dp", "tensor"),
            P("dp", "tensor"),
            P("tensor", "dp"),
        ),
        check_vma=False,
    )
```

```python
import functools
import math

import jax
import jax.numpy as jnp
from jax import lax
from jax.experimental import pallas as pl
from jax.experimental.pallas import tpu as pltpu
from jax.sharding import PartitionSpec as P

HD = 128
E4_TOP = 448.0
E5_TOP = 57344.0
BF = jnp.bfloat16
F32 = jnp.float32
MESH = pl.DeviceIdType.MESH
NZ, NX, TOK, FEAT, QC, KC = 8, 4, 128, 512, 256, 32
DIRS = (1, -1)


def nn(a, b):
    return jnp.dot(a, b, preferred_element_type=F32)


def nt(a, b):
    return lax.dot_general(a, b, (((1,), (1,)), ((), ())), preferred_element_type=F32)


def halves(a):
    high = a.astype(BF)
    return high, (a - high.astype(F32)).astype(BF)


def precise(dot, a, b):
    ah, al = halves(a)
    bh, bl = halves(b)
    return dot(ah, bh) + (dot(ah, bl) + dot(al, bh))


def power_of_half(e):
    out = jnp.float32(1.0)
    for bit in range(5):
        out = out * jnp.where(((e >> bit) & 1) == 1, jnp.float32(2.0 ** -(1 << bit)), jnp.float32(1.0))
    return out


def clip(v, limit):
    return jnp.minimum(jnp.maximum(v, -limit), limit)


def rot(v, c, s):
    return jnp.concatenate([v[:64] * c - v[64:] * s, v[64:] * c + v[:64] * s], axis=0)


def unrot(v, c, s):
    return jnp.concatenate([v[:64] * c + v[64:] * s, v[64:] * c - v[:64] * s], axis=0)


ORDER = (
    0, 46, 3, 13, 1, 15, 5, 2, 4, 14, 19, 47, 8, 131, 55, 65, 6, 16, 9, 23, 70, 75, 18, 100, 60,
    86, 105, 7, 10, 21, 71, 121, 61, 95, 96, 76, 81, 106, 116, 17, 20, 85, 126, 91, 11, 80, 36,
    110, 66, 101, 56, 26, 57, 111, 38, 67, 28, 62, 115, 12, 22, 90, 27, 37, 42, 125, 29, 39, 72,
    77, 32, 120, 30, 33, 44, 130, 48, 40, 25, 24, 97, 49, 87, 34, 82, 43, 35, 45, 92, 41, 31, 102,
    122, 107, 127, 50, 118, 108, 103, 133, 113, 98, 141, 138, 128, 152, 93, 123, 132, 117, 112, 52,
    53, 151, 140, 51, 83, 58, 78, 63, 88, 68, 150, 139, 143, 73, 154, 153, 142, 193, 186, 194, 195,
    188, 187, 54, 134, 163, 129, 175, 94, 124, 164, 119, 176, 114, 165, 89, 84, 109, 177, 104, 166,
    79, 74, 197, 99, 64, 137, 136, 69, 59, 196, 158, 144, 135, 178, 167, 168, 203, 190, 204, 147,
    179, 155, 189, 202, 198, 199, 159, 145, 201, 180, 161, 162, 208, 169, 183, 192, 172, 191, 148,
    156, 146, 160, 181, 170, 184, 173, 200, 157, 149, 207, 182, 171, 185, 174, 205, 206, 209, 210,
)


def kernel(
    scale_ref, loss_ref, tok_hbm, gain_hbm, pos_hbm, og_hbm, wq_hbm, wk_hbm, wv_hbm, wo_hbm,
    mixed_hbm, dtok_hbm, gq_hbm, gkv_hbm, go_hbm,
    mixed_out, dtok_out, gq_out, go_out, gkv_out,
    wq, wkt, wvt, wkv, wo, toks, acts, gout, pgout,
    pm, rm, pd, rd,
    sgo, xgo, ygo, actr, dqr, dkr_all, w_send, w_own, w_far, v_send, v_own, v_far,
    att_own, att_far, dq_own, dk_own, probs, q_rot, k_rot, v_rows, lane_inv,
    angles, projected, scaled_rows, gain_ref, pos_ref,
    mg, kvs, kvr, dks, dkr, pr,
    qacc, kvacc, dacc,
    load_sem, out_sem, gt_s, gt_r, gg_s, gg_r, zm_s, zm_r, zd_s, zd_r, xo_s, xo_r,
    aa_s, aa_r, dq_s, dq_r, dk_s, dk_r, sm_s, sm_r, cp_s, cp_r,
):
    dp = lax.axis_index("dp")
    me = lax.axis_index("tensor")
    z, yh = me // 2, lax.rem(me, 2)
    x, yl, core = dp // 4, lax.rem(dp // 2, 2), lax.rem(dp, 2)
    sent = []
    tasks = {}
    K_ORDER = (1, 0)
    SLOTS = [(d, k, g) for k in (0, 1) for d in range(5) for g in (DIRS if 0 < d < 4 else (1,))]

    def name(head, *parts):
        return head + ",".join(("+" if v > 0 else "-") if n == len(parts) - 1 else str(v) for n, v in enumerate(parts))

    def task(key, *steps):
        tasks[key] = steps

    def call(f, *args):
        return functools.partial(f, *args)

    def copy(src, dst, ssem, rsem, **where):
        return pltpu.make_async_remote_copy(
            src_ref=src, dst_ref=dst, send_sem=ssem, recv_sem=rsem,
            device_id=where, device_id_type=MESH,
        )

    def push(*args, **where):
        c = copy(*args, **where)
        c.start()
        sent.append(c)

    def zdev(sign):
        return lax.rem(z + sign + NZ, NZ) * 2 + yh

    def xdev(sign):
        return lax.rem(x + sign + NX, NX) * 4 + yl * 2 + core

    ypart = z * 2 + (1 - yh)
    ylpart = x * 4 + (1 - yl) * 2 + core
    cpart = x * 4 + yl * 2 + (1 - core)

    def near(n, sign):
        return lax.rem(x + sign * (n // 2) + NX, NX), (core if n % 2 == 0 else 1 - core)

    def near_dp(n, sign):
        xs, cs = near(n, sign)
        return xs * 4 + yl * 2 + cs

    first_load = pltpu.make_async_copy(tok_hbm.at[0], toks.at[z, yh], load_sem.at[4])
    first_load.start()
    loads = [
        pltpu.make_async_copy(wk_hbm, wkt, load_sem.at[0]),
        pltpu.make_async_copy(wv_hbm, wvt, load_sem.at[1]),
        pltpu.make_async_copy(wq_hbm, wq, load_sem.at[2]),
        pltpu.make_async_copy(wo_hbm, wo, load_sem.at[3]),
    ]
    grad_load = pltpu.make_async_copy(og_hbm.at[0], gout.at[z, yh], load_sem.at[5])
    gain_load = pltpu.make_async_copy(gain_hbm, gain_ref, load_sem.at[6])
    pos_load = pltpu.make_async_copy(pos_hbm, pos_ref, load_sem.at[7])
    grad_load.start()
    gain_load.start()
    pos_load.start()
    for c in loads:
        c.start()

    barrier = pltpu.get_barrier_semaphore()

    def greet(o, carry):
        pl.semaphore_signal(
            barrier, inc=1, device_id={"tensor": lax.rem(me + o, 16)}, device_id_type=MESH
        )
        return carry

    lax.fori_loop(1, 16, greet, 0)
    for other in [near_dp(n, 1) for n in range(1, 8)] + [ylpart]:
        pl.semaphore_signal(barrier, inc=1, device_id={"dp": other}, device_id_type=MESH)

    lims = [E4_TOP * power_of_half(scale_ref[i]) for i in range(6)]
    glim = E5_TOP * power_of_half(scale_ref[6] + loss_ref[0])

    def as_row(column):
        return jnp.broadcast_to(column, (TOK, 128)).T

    first_load.wait()
    pl.semaphore_wait(barrier, 23)

    def spot(zz, k):
        return lax.rem(zz + NZ, NZ), (yh if k == 0 else 1 - yh)

    def half_of(sign):
        return pl.ds(0 if sign > 0 else TOK // 2, TOK // 2)

    def gather(p, buf, ss, rs, prepare=None):
        def part(zz, k, h):
            zs, ys = spot(zz, k)
            return buf.at[zs, ys, pl.ds(h * 64, 64)]

        def carried(g):
            return 0 if g > 0 else 1

        first = {(1, 0): 0, (2, 0): 4, (3, 0): 8, (4, 0): 12, (1, 1): 14, (2, 1): 18}

        def ring(d, k, g, h):
            i = first[d, k] + (0 if g > 0 else 1)
            return i if (d, k) in ((4, 0), (2, 1)) else i + 2 * h

        def send(d, k, g, h):
            v, i = part(z - g * (d - 1), k, h), ring(d, k, g, h)
            push(v, v, ss.at[i], rs.at[i], tensor=zdev(g))

        def wait(d, k, g, h):
            v, i = part(z - g * d, k, h), ring(d, k, g, h)
            copy(v, v, ss.at[i], rs.at[i], tensor=zdev(g)).wait_recv()

        def side(d, g, h):
            if d == 0:
                return 20 + h
            return {2: 22, 3: 24, 4: 28}[d] + (0 if g > 0 else 1) + (2 * h if d == 3 else 0)

        def send_side(d, g, h):
            v, i = part(z - g * d, 0, h), side(d, g, h)
            push(v, v, ss.at[i], rs.at[i], tensor=ypart)

        def wait_side(d, g, h):
            v, i = part(z - g * d, 1, h), side(d, g, h)
            copy(v, v, ss.at[i], rs.at[i], tensor=ypart).wait_recv()

        def begin():
            if prepare is not None:
                prepare()
            for h in (0, 1):
                send_side(0, 1, h)
                for g in DIRS:
                    send(1, 0, g, h)

        def partner(h):
            wait_side(0, 1, h)
            for g in DIRS:
                send(1, 1, g, h)

        task(p + "0", begin)
        for h in (0, 1):
            task(p + "f11%d" % h, call(partner, h))
        for g in DIRS:
            n = "+" if g > 0 else "-"
            c = carried(g)
            for h in (0, 1):
                task(p + "f20%s%d" % (n, h), call(wait, 1, 0, g, h), call(send, 2, 0, g, h))
                task(p + "f30%s%d" % (n, h), call(wait, 2, 0, g, h), call(send, 3, 0, g, h))
            task(p + "f40" + n, call(wait, 3, 0, g, c), call(send, 4, 0, g, c))
            task(p + "f21" + n, call(wait, 1, 1, g, c), call(send, 2, 1, g, c))
            task(p + "s2" + n, call(send_side, 2, g, 1 - c))
            task(p + "s3%s%d" % (n, c), call(send_side, 3, g, c))
            task(p + "s3%s%d" % (n, 1 - c), call(wait, 3, 0, g, 1 - c), call(send_side, 3, g, 1 - c))
            task(p + "s4" + n, call(wait, 4, 0, g, c), call(send_side, 4, g, c))

        def arrived(d, k, g):
            c = carried(g)
            if (d, k) == (1, 1):
                wait(1, 1, g, 1 - c)
            elif (d, k) == (2, 1):
                wait(2, 1, g, c)
                wait_side(2, g, 1 - c)
            elif (d, k) == (3, 1):
                wait_side(3, g, 0)
                wait_side(3, g, 1)
            elif (d, k) == (4, 1):
                for other in DIRS:
                    wait_side(4, other, carried(other))

        return arrived

    def exchange(src, dst, j):
        def start(o, carry):
            peer = lax.rem(me + o, 16)
            copy(src(peer), dst.at[me], sm_s.at[j, o], sm_r.at[j, o], tensor=peer).start()
            return carry

        def recv(o, carry):
            origin = lax.rem(me + 16 - o, 16)
            copy(src(me), dst.at[origin], sm_s.at[j, o], sm_r.at[j, o], tensor=origin).wait_recv()
            return carry

        def drain(o, carry):
            peer = lax.rem(me + o, 16)
            copy(src(peer), dst.at[me], sm_s.at[j, o], sm_r.at[j, o], tensor=peer).wait_send()
            return carry

        return (
            lambda: lax.fori_loop(1, 16, start, 0),
            lambda: lax.fori_loop(1, 16, recv, 0),
            lambda: lax.fori_loop(1, 16, drain, 0),
        )

    mg_start, mg_wait, mg_drain = exchange(lambda peer: mg.at[me], mg, 0)
    kv_start, kv_wait, kv_drain = exchange(lambda peer: kvs.at[peer // 4], kvr, 1)
    dk_start, dk_wait, dk_drain = exchange(lambda peer: dks.at[peer], dkr, 2)
    pr_start, pr_wait, pr_drain = exchange(lambda peer: pr.at[me], pr, 3)

    t_arrived = gather("T", toks, gt_s, gt_r)

    def cast_grad():
        grad_load.wait()
        gout[z, yh] = clip(gout[z, yh].astype(F32), glim).astype(BF)

    g_arrived = gather("G", gout, gg_s, gg_r, cast_grad)

    def send_squares():
        gain_load.wait()
        gain = gain_ref[...].astype(F32).reshape(1, FEAT)
        lanes = [gain[:, i * 128 : (i + 1) * 128] for i in range(4)]
        rows = toks[z, yh].astype(F32)
        squares = as_row(jnp.sum(rows * rows, axis=1, keepdims=True))[:4]
        mg[me] = jnp.concatenate(lanes + [squares], axis=0)
        mg_start()

    task("mg", send_squares)

    def gain_of(slot):
        g = mg[slot]
        return jnp.concatenate([g[i : i + 1] for i in range(4)], axis=1)

    def prepare():
        pos_load.wait()
        pair = lax.broadcasted_iota(jnp.int32, (64, TOK), 0).astype(F32)
        angle = pos_ref[...].astype(F32) * jnp.exp(pair * (-2.0 * math.log(500000.0) / HD))
        angles[0] = jnp.cos(angle)
        angles[1] = jnp.sin(angle)
        for total in (qacc, kvacc, dacc, projected):
            total[...] = jnp.zeros_like(total)
        mg_wait()
        squares = jnp.sum(mg[...], axis=0)[4:5]
        inv_row = lax.rsqrt(squares / (FEAT * 16) + 1e-05)
        lane_inv[...] = jnp.broadcast_to(inv_row[:1], (128, TOK)).T
        for c in loads:
            c.wait()

    task("pre", prepare)

    def block(d, k, g):
        zs, ys = spot(z - g * d, k)
        return zs, ys, pl.ds(pl.multiple_of((zs * 2 + ys) * 512, 512), 512)

    def act_copy(zs, ys):
        return copy(
            acts.at[zs, ys], actr.at[x * 2 + core, lax.rem(zs, 2)],
            aa_s.at[zs * 2 + ys], aa_r.at[(x * 2 + core) * 2 + lax.rem(zs, 2)],
            dp=(zs // 2) * 4 + yl * 2 + ys,
        )

    def project(d, k, g):
        t_arrived(d, k, g)
        zs, ys, r = block(d, k, g)
        inv = lane_inv[:, pl.ds(0, 1)]
        a = toks[zs, ys].astype(F32) * inv * gain_of(zs * 2 + ys)
        a = clip(a, lims[0]).astype(BF)
        acts[zs, ys] = a

        @pl.when(jnp.logical_or(zs // 2 != x, ys != core))
        def _():
            act_copy(zs, ys).start()

        w = clip(wq[r, :].astype(F32), lims[1]).astype(BF)
        wq[r, :] = w
        wn = jnp.concatenate(
            [clip(wkt[:, r].astype(F32), lims[2]), clip(wvt[:, r].astype(F32), lims[3])], axis=0
        ).T.astype(BF)
        wkv[r, :] = wn
        qacc[...] += nn(a, w)
        kvacc[...] += nn(a, wn)

    def cast_out(d, k, g):
        zs, ys, r = block(d, k, g)
        wo[:, r] = clip(wo[:, r].astype(F32), lims[4]).astype(BF)

    def back(d, k, g):
        g_arrived(d, k, g)
        zs, ys, r = block(d, k, g)
        dacc[...] += nt(wo[:, r], gout[zs, ys])

    def natural(i):
        low = i & 31
        return (low & 3) * 16 + (i >> 5) * 8 + (low >> 2)

    i0 = lax.broadcasted_iota(jnp.int32, (64, 64), 0)
    i1 = lax.broadcasted_iota(jnp.int32, (64, 64), 1)

    def send_kv():
        by_head = jnp.where(natural(i1) == i0, 1.0, 0.0).astype(BF)
        kvs[...] = nt(by_head, kvacc[...].astype(BF)).astype(BF).reshape(4, 16, TOK)
        kv_start()
        kvr[me] = kvs[me // 4]

    task("kv", send_kv)

    def turn_query():
        q_t = qacc[...].astype(BF).astype(F32).T
        for h in range(2):
            q_rot[h] = rot(q_t[h * HD : (h + 1) * HD], angles[0], angles[1])

    task("qrot", turn_query)

    def attend():
        kv_wait()
        kv = kvr[...].astype(F32)
        k_t = kv[:, :8].reshape(HD, TOK)
        v_t = kv[:, 8:].reshape(HD, TOK)
        k_turned = rot(k_t, angles[0], angles[1])
        k_rot[...] = k_turned
        k_rows = k_turned.T
        v_t16 = v_t.astype(BF)
        v_rows[...] = v_t.T.astype(BF)
        src = lax.broadcasted_iota(jnp.int32, (TOK, TOK), 0)
        dst = lax.broadcasted_iota(jnp.int32, (TOK, TOK), 1)
        allowed = (src <= dst) & (src >= dst - pos_ref[...])
        for h in range(2):
            score = precise(nn, k_rows, q_rot[h]) * (1.0 / math.sqrt(HD))
            weight = jnp.where(allowed, jnp.exp(jnp.where(allowed, score, 0.0)), 0.0)
            p = weight / jnp.sum(weight, axis=0, keepdims=True)
            probs[h] = p
            att = nn(v_t16, p.astype(BF)).astype(BF).astype(F32)
            att_own[pl.ds(h * HD, HD), :] = clip(att, lims[5]).astype(BF)
        push(att_own, att_far, cp_s.at[1], cp_r.at[1], dp=cpart)

    task("att", attend)

    def mix(d, k, g):
        zs, ys, r = block(d, k, -g)
        att_rows = att_own[...].astype(F32).T.astype(BF)
        pm[zs, ys] = nn(att_rows, wo[:, r]).astype(BF)

    def share_gout():
        push(gout.at[:, 1 - core], pgout, cp_s.at[2], cp_r.at[2], dp=cpart)

    task("gpush", share_gout)

    def score_grad(h):
        g = dacc[pl.ds(h * HD, HD), :].astype(BF)
        dw = nn(v_rows[...], g)
        p = probs[h]
        delta = jnp.sum(p * dw, axis=0, keepdims=True)
        return g, p, p * (dw - delta) * (1.0 / math.sqrt(HD))

    def backward():
        dk_rot = jnp.zeros((HD, TOK), F32)
        dv_t = jnp.zeros((HD, TOK), F32)
        for h in range(2):
            g, p, ds = score_grad(h)
            p_high, p_low = halves(p)
            dv_t = dv_t + nt(g, p_high) + nt(g, p_low)
            dk_rot = dk_rot + precise(nt, q_rot[h], ds)
            probs[h] = ds
        dk_t = unrot(dk_rot, angles[0], angles[1])
        dks[...] = jnp.concatenate(
            [dk_t.reshape(16, 8, TOK), dv_t.reshape(16, 8, TOK)], axis=1
        ).astype(BF)
        dk_start()
        dkr[me] = dks[me]

    task("bwd", backward)

    def to_row(src, to, ss, rs):
        for n in range(1, 8):
            push(src, to.at[x * 2 + core], ss.at[n], rs.at[n], dp=near_dp(n, 1))

    def query_grad():
        for h in range(2):
            dq = unrot(precise(nn, k_rot[...], probs[h]), angles[0], angles[1])
            dq_own[pl.ds(h * HD, HD), :] = dq.astype(BF)
        to_row(dq_own, dqr, dq_s, dq_r)

    task("bwq", query_grad)

    def key_grad():
        dk_wait()
        by_column = jnp.where(natural(i0) == i1, 1.0, 0.0).astype(BF)
        dkv = jnp.sum(dkr[...].astype(F32).reshape(4, 4, 16, TOK), axis=1).reshape(64, TOK)
        dk_own[...] = nn(by_column, dkv.astype(BF)).astype(BF)
        to_row(dk_own, dkr_all, dk_s, dk_r)

    task("dkfin", key_grad)

    def down(d, k, g):
        zs, ys, r = block(d, k, -g)
        term = (nn(wq[r, :], dq_own[...]) + nn(wkv[r, :], dk_own[...])).astype(BF)
        pd[zs, ys] = term
        high, low = halves(toks[zs, ys].astype(F32) * gain_of(zs * 2 + ys))
        projected[...] += nn(high, term) + nn(low, term)

    for d, k, g in SLOTS:
        task(name("proj", d, k, g), call(project, d, k, g))
        task(name("clipo", d, k, g), call(cast_out, d, k, g))
        task(name("back", d, k, g), call(back, d, k, g))
        task(name("mix", d, k, g), call(mix, d, k, g))
        task(name("down", d, k, g), call(down, d, k, g))

    def send_product():
        diagonal = lax.broadcasted_iota(jnp.int32, (TOK, TOK), 0) == lax.broadcasted_iota(
            jnp.int32, (TOK, TOK), 1
        )
        own = jnp.sum(jnp.where(diagonal, projected[...], 0.0), axis=0, keepdims=True)
        pr[me] = jnp.broadcast_to(own, (8, TOK))
        pr_start()

    task("prx", send_product)

    def scatter(q, p, r, ss, rs):
        half = p.shape[2] // 2
        first = {(3, 1): 0, (4, 1): 2, (1, 0): 6, (2, 0): 8, (3, 0): 12, (4, 0): 16}

        def area(h):
            return pl.ds(h * half, half)

        def place(d, k, g):
            return spot(z + g * d, k)

        def ring(st, k, g, h):
            i = first[st, k] + (0 if g > 0 else 1)
            return i if (st, k) in ((3, 1), (1, 0)) else i + 2 * h

        def side(d, g, h):
            if d in (0, 4):
                return (28 if d == 0 else 20) + h
            return {3: 22, 2: 26}[d] + (0 if g > 0 else 1) + (2 * h if d == 3 else 0)

        def send(st, k, g, h):
            zs, ys = place(5 - st, k, g)
            i = ring(st, k, g, h)
            push(p.at[zs, ys, area(h)], r.at[i], ss.at[i], rs.at[i], tensor=zdev(g))

        def send_side(d, g, h):
            zs, ys = place(d, 1, g)
            i = side(d, g, h)
            push(p.at[zs, ys, area(h)], r.at[i], ss.at[i], rs.at[i], tensor=ypart)

        def got(st, k, g, h):
            i = ring(st, k, g, h)
            copy(r.at[i], r.at[i], ss.at[i], rs.at[i], tensor=zdev(g)).wait_recv()
            return r[i].astype(F32)

        def got_side(d, g, h):
            i = side(d, g, h)
            copy(r.at[i], r.at[i], ss.at[i], rs.at[i], tensor=ypart).wait_recv()
            return r[i].astype(F32)

        def add(d, k, g, h, *terms):
            zs, ys = place(d, k, g)
            total = p[zs, ys, area(h)].astype(F32)
            for t in terms:
                total = total + t()
            p[zs, ys, area(h)] = total.astype(BF)

        def pieces(k, h):
            return [call(got, 4, k, g, h) for g in DIRS]

        for h in (0, 1):
            task(q + "cross%d" % h, call(add, 0, 1, 1, h, *pieces(1, h)), call(send_side, 0, 1, h))
        task(q + "side4", call(send_side, 4, 1, 0), call(send_side, 4, 1, 1))
        for g in DIRS:
            n = "+" if g > 0 else "-"
            c = 0 if g > 0 else 1
            o = 1 - c
            task(q + "side3" + n, call(send_side, 3, g, c), call(send_side, 3, g, o))
            task(q + "side2" + n, call(send, 3, 1, g, c), call(send_side, 2, g, o))
            task(q + "near%s%d" % (n, o), call(send, 4, 1, g, o))
            task(
                q + "near%s%d" % (n, c),
                call(add, 1, 1, g, c, call(got, 3, 1, g, c)), call(send, 4, 1, g, c),
            )
            task(
                q + "first" + n,
                call(add, 4, 0, g, c, call(got_side, 4, 1, c)), call(send, 1, 0, g, c),
            )
            for h in (0, 1):
                terms = [call(got_side, 3, g, h)] + ([call(got, 1, 0, g, h)] if h == c else [])
                task(
                    q + "step1%s%d" % (n, h), call(add, 3, 0, g, h, *terms), call(send, 2, 0, g, h)
                )
                terms = [call(got, 2, 0, g, h)] + ([call(got_side, 2, g, h)] if h == o else [])
                task(
                    q + "step2%s%d" % (n, h), call(add, 2, 0, g, h, *terms), call(send, 3, 0, g, h)
                )
                task(
                    q + "step3%s%d" % (n, h),
                    call(add, 1, 0, g, h, call(got, 3, 0, g, h)), call(send, 4, 0, g, h),
                )

        def finish():
            total = []
            for h in (0, 1):
                t = p[z, yh, area(h)].astype(F32)
                for piece in pieces(0, h) + [call(got_side, 0, 1, h)]:
                    t = t + piece()
                total.append(t)
            return jnp.concatenate(total, axis=0)

        return finish

    def group_sum(q, make, p, r, y, ss, rs):
        rows_n = p.shape[1]
        half = rows_n // 2

        def where(xx, k):
            return lax.rem(xx + NX, NX) * 2 + (yl if k == 0 else 1 - yl)

        def number(st, k, sign):
            return (st - 1) * 4 + k * 2 + (0 if sign > 0 else 1)

        def ends(st, k, sign):
            to = r.at[0 if sign > 0 else 1, st - 1, k]
            return to.at[pl.ds(0 if sign > 0 else half, half)] if st == 1 else to

        def send(st, k, sign):
            v = p.at[where(x + sign * (3 - st), k)]
            if st == 1:
                v = v.at[pl.ds(0 if sign > 0 else half, half)]
            i = number(st, k, sign)
            push(v, ends(st, k, sign), ss.at[i], rs.at[i], dp=xdev(sign))

        def wait(st, k, sign):
            v = ends(st, k, sign)
            i = number(st, k, sign)
            copy(v, v, ss.at[i], rs.at[i], dp=xdev(sign)).wait_recv()

        def step(k, sign):
            wait(1, k, sign)
            s = where(x + sign, k)
            a = pl.ds(0 if sign > 0 else half, half)
            j = 0 if sign > 0 else 1
            p[s, a] = (p[s, a].astype(F32) + r[j, 0, k, a].astype(F32)).astype(BF)
            send(2, k, sign)

        def total(k):
            for sign in DIRS:
                wait(2, k, sign)
            return p[where(x, k)].astype(F32) + (r[0, 1, k].astype(F32) + r[1, 1, k].astype(F32))

        def cross():
            p[where(x, 1)] = total(1).astype(BF)
            push(p.at[where(x, 1)], y, ss.at[8], rs.at[8], dp=ylpart)

        def finish():
            own = total(0)
            copy(y, y, ss.at[8], rs.at[8], dp=ylpart).wait_recv()
            return own + y[...].astype(F32)

        def start(k):
            for g in DIRS:
                send(1, k, g)

        for k in (0, 1):
            for dx in (2, 1, -1, 0):
                task(q + "g%d,%d" % (dx, k), call(lambda dx, k: make(where(x + dx, k)), dx, k))
            task(q + "send1,%d" % k, call(start, k))
            for g in DIRS:
                task(name(q + "step,", k, g), call(step, k, g))
        task(q + "cross", cross)
        return finish

    m_finish = scatter("M", pm, rm, zm_s, zm_r)
    n_finish = scatter("N", pd, rd, zd_s, zd_r)

    waited = set()

    def once(key, src, dst, i):
        if key not in waited:
            waited.add(key)
            copy(src, dst, cp_s.at[i], cp_r.at[i], dp=cpart).wait_recv()

    def out_grads(s):
        once("gout", pgout, pgout, 2)
        once("att", att_far, att_far, 1)
        sgo[s] = (nn(att_own[...], gout[s, core]) + nn(att_far[...], pgout[s])).astype(BF)

    def act_wait():
        if "acts" not in waited:
            waited.add("acts")
            for n in range(1, 8):
                xs, cs = near(n, -1)
                for side in (0, 1):
                    v = actr.at[xs * 2 + cs, side]
                    i = (xs * 2 + cs) * 2 + side
                    copy(v, v, aa_s.at[n], aa_r.at[i], dp=near_dp(n, -1)).wait_recv()

    def row_sum(q, own, to, ss, rs, out, keep, far, i):
        def product(side):
            act_wait()
            total = nn(own[...], acts[x * 2 + side, core])
            for n in range(1, 8):
                xs, cs = near(n, -1)
                v = to.at[xs * 2 + cs]
                if (q, n) not in waited:
                    waited.add((q, n))
                    copy(v, v, ss.at[n], rs.at[n], dp=near_dp(n, -1)).wait_recv()
                total = total + nn(to[xs * 2 + cs], actr[xs * 2 + cs, side])
            return total

        def give():
            out[...] = product(1 - yl).astype(BF)
            push(out, far, cp_s.at[i], cp_r.at[i], dp=ylpart)

        def hold():
            keep[...] = product(yl)

        def finish():
            copy(far, far, cp_s.at[i], cp_r.at[i], dp=ylpart).wait_recv()
            return keep[...] + far[...].astype(F32)

        task(q + "1", give)
        task(q + "0", hold)
        return finish

    o_finish = group_sum("O", out_grads, sgo, xgo, ygo, xo_s, xo_r)
    w_finish = row_sum("W", dq_own, dqr, dq_s, dq_r, w_send, w_own, w_far, 3)
    v_finish = row_sum("V", dk_own, dkr_all, dk_s, dk_r, v_send, v_own, v_far, 4)

    outs = []

    def emit(src, to):
        c = pltpu.make_async_copy(src, to, out_sem.at[len(outs)])
        c.start()
        outs.append(c)

    def end_mixed():
        mixed_out[0] = m_finish().astype(BF)
        emit(mixed_out, mixed_hbm)

    def end_out():
        go_out[...] = o_finish()
        emit(go_out, go_hbm)

    def end_query():
        gq_out[...] = w_finish().T
        emit(gq_out, gq_hbm)

    def end_key():
        gkv_out[...] = v_finish()
        emit(gkv_out, gkv_hbm)

    def end_down():
        scaled_rows[...] = n_finish().T * gain_of(me)

    def end_tokens():
        pr_wait()
        inv = lane_inv[:, pl.ds(0, 1)]
        proj = jnp.broadcast_to(jnp.sum(pr[...], axis=0)[:1], (128, TOK)).T[:, :1]
        slope = inv * inv * inv * proj / (FEAT * 16)
        dtok_out[0] = (inv * scaled_rows[...] - toks[z, yh].astype(F32) * slope).astype(BF)
        emit(dtok_out, dtok_hbm)

    task("Mfin", end_mixed)
    task("Ofin", end_out)
    task("Wfin", end_query)
    task("Vfin", end_key)
    task("Nfin", end_down)
    task("out", end_tokens)

    def act_drain(slot, carry):
        @pl.when(jnp.logical_or(slot // 4 != x, lax.rem(slot, 2) != core))
        def _():
            act_copy(slot // 2, lax.rem(slot, 2)).wait_send()

        return carry

    listed = list(tasks.values())
    assert sorted(ORDER) == list(range(len(listed)))
    names = list(tasks)
    idle = {"att", "dkfin", "Nfin"} | {key for key in names if key.startswith(("Nstep", "Ncross"))}
    begun = []
    for number in ORDER:
        if names[number] in idle:
            while begun and len(sent) - begun[0] > 24:
                sent_first = begun.pop(0)
                sent[sent_first].wait_send()
        if names[number] == "att":
            mg_drain()
        if names[number] == "dkfin":
            kv_drain()
            lax.fori_loop(0, 16, act_drain, 0)
        if names[number] == "Nfin":
            dk_drain()
        before = len(sent)
        for step in listed[number]:
            step()
        begun.extend(range(before, len(sent)))

    for i in begun:
        sent[i].wait_send()
    pr_drain()
    for c in outs:
        c.wait()


def spread(*refs):
    ins, outs, held, got, put = refs[:5], refs[5:11], refs[11:16], refs[16], refs[17]
    reads = [pltpu.make_async_copy(a, b, got.at[i]) for i, (a, b) in enumerate(zip(ins, held))]
    parts = [(0, held[0]), (1, held[1]), (2, held[2]), (4, held[4])]
    parts += [(3, held[3].at[pl.ds(0, KC)]), (3, held[3].at[pl.ds(KC, KC)])]
    places = (outs[0], outs[1], outs[2], outs[5], outs[3], outs[4])
    for c in reads:
        c.start()
    writes = []
    done = set()
    for i, ((source, view), to) in enumerate(zip(parts, places)):
        if source not in done:
            done.add(source)
            reads[source].wait()
        writes.append(pltpu.make_async_copy(view, to, put.at[i]))
        writes[-1].start()
    for c in writes:
        c.wait()


def body(
    tokens, norm_gain, w_query, w_key, w_value, w_output, positions, scale_exps, loss_exp, out_grad
):
    vmem = pl.BlockSpec(memory_space=pltpu.VMEM)
    smem = pl.BlockSpec(memory_space=pltpu.SMEM)
    hbm = pl.BlockSpec(memory_space=pl.ANY)
    V = pltpu.VMEM
    dma = pltpu.SemaphoreType.DMA
    S = jax.ShapeDtypeStruct
    sums = [V((8, 2, TOK, FEAT), BF), V((30, TOK // 2, FEAT), BF)]
    sums_down = [V((8, 2, FEAT, TOK), BF), V((30, FEAT // 2, TOK), BF)]

    def by_group(n):
        return V((8, n, FEAT), BF), V((2, 2, 2, n, FEAT), BF), V((n, FEAT), BF)

    parts = pl.pallas_call(
        kernel,
        out_shape=(
            S((1, TOK, FEAT), BF), S((1, TOK, FEAT), BF), S((FEAT, QC), F32),
            S((2 * KC, FEAT), F32), S((QC, FEAT), F32),
        ),
        in_specs=[smem, smem] + [hbm] * 8,
        out_specs=(hbm,) * 5,
        scratch_shapes=[
            V((1, TOK, FEAT), BF), V((1, TOK, FEAT), BF), V((FEAT, QC), F32), V((QC, FEAT), F32),
            V((2 * KC, FEAT), F32),
            V((8192, QC), BF), V((KC, 8192), BF), V((KC, 8192), BF), V((8192, 2 * KC), BF),
            V((QC, 8192), BF),
            V((8, 2, TOK, FEAT), BF), V((8, 2, TOK, FEAT), BF), V((8, 2, TOK, FEAT), BF),
            V((8, TOK, FEAT), BF),
            *sums, *sums_down,
            *by_group(QC),
            V((8, 2, TOK, FEAT), BF), V((8, QC, TOK), BF), V((8, 64, TOK), BF),
            V((QC, FEAT), BF), V((QC, FEAT), F32), V((QC, FEAT), BF),
            V((64, FEAT), BF), V((64, FEAT), F32), V((64, FEAT), BF),
            V((QC, TOK), BF), V((QC, TOK), BF), V((QC, TOK), BF), V((64, TOK), BF),
            V((2, TOK, TOK), F32), V((2, HD, TOK), F32), V((HD, TOK), F32), V((TOK, HD), BF),
            V((TOK, 128), F32), V((2, 64, TOK), F32), V((TOK, TOK), F32), V((TOK, FEAT), F32),
            V((FEAT,), BF), V((1, TOK), jnp.int32),
            V((16, 8, 128), F32), V((4, 16, TOK), BF), V((16, 16, TOK), BF),
            V((16, 16, TOK), BF), V((16, 16, TOK), BF), V((16, 8, TOK), F32),
            V((TOK, QC), F32), V((TOK, 2 * KC), F32), V((QC, TOK), F32),
            dma((8,)), dma((5,)),
            dma((30,)), dma((30,)), dma((30,)), dma((30,)),
            dma((30,)), dma((30,)), dma((30,)), dma((30,)),
            dma((9,)), dma((9,)), dma((16,)), dma((16,)), dma((8,)), dma((8,)), dma((8,)), dma((8,)),
            dma((4, 16)), dma((4, 16)), dma((5,)), dma((5,)),
        ],
        compiler_params=pltpu.CompilerParams(
            collective_id=0, has_side_effects=True, vmem_limit_bytes=60 * 1024 * 1024
        ),
    )(
        scale_exps, loss_exp, tokens, norm_gain, positions, out_grad,
        w_query, w_key.T, w_value.T, w_output,
    )
    mixed, d_rows, grad_query, grad_key, grad_value, grad_output = pl.pallas_call(
        spread,
        out_shape=(
            S((1, TOK, FEAT), BF), S((1, TOK, FEAT), BF), S((FEAT, QC), F32),
            S((KC, FEAT), F32), S((KC, FEAT), F32), S((QC, FEAT), F32),
        ),
        in_specs=[hbm] * 5,
        out_specs=(hbm,) * 6,
        scratch_shapes=[
            V((1, TOK, FEAT), BF), V((1, TOK, FEAT), BF), V((FEAT, QC), F32),
            V((2 * KC, FEAT), F32), V((QC, FEAT), F32), dma((5,)), dma((6,)),
        ],
        compiler_params=pltpu.CompilerParams(vmem_limit_bytes=60 * 1024 * 1024),
    )(*parts)
    return mixed, d_rows, grad_query, grad_key.T, grad_value.T, grad_output


def solution(mesh):
    placed = (
        P("dp", None, "tensor"),
        P("tensor"),
        P(None, "tensor"),
        P(None, "tensor"),
        P(None, "tensor"),
        P("tensor", None),
        P("dp", None),
        P(),
        P(),
        P("dp", None, "tensor"),
    )
    return jax.shard_map(
        body,
        mesh=mesh,
        in_specs=placed,
        out_specs=(
            P("dp", None, "tensor"),
            P("dp", None, "tensor"),
            P("dp", "tensor"),
            P("dp", "tensor"),
            P("dp", "tensor"),
            P("tensor", "dp"),
        ),
        check_vma=False,
    )
```
